32 devices in a mesh: ctx: 4 (over y, x), ch: 8 (over z, core).
Axes of the slice: x: 2, y: 2, z: 4, core: 2. Of those that a mesh axis runs over, the one named last changes fastest.
Arguments:
- features: bfloat16 [3, 512, 8192], P(None, 'ctx', 'ch'), may hold values from -6 to 6
- short_kernel: float32 [3, 7, 8192], P(None, None, 'ch'), may hold values from -2 to 2
- long_filter: bfloat16 [512, 8192], P('ctx', 'ch'), may hold values from -0.25 to 0.25
- out_weight: bfloat16 [8192, 8192], P(None, 'ch'), may hold values from -0.0625 to 0.0625
- grad_out: bfloat16 [512, 8192], P('ctx', 'ch'), may hold values from -6 to 6
Outputs:
- grad_features: bfloat16 [3, 512, 8192], P(None, 'ctx', 'ch')
- grad_kernel: float32 [3, 7, 8192], P(None, None, 'ch')
- grad_filter: float32 [512, 8192], P('ctx', 'ch')
- grad_weight: float32 [8192, 8192], P('ctx', 'ch')
The draws below stay inside these ranges and needn't reach their ends.
All inputs are finite; a program needn't handle non-finite values.
Results may differ from the reference program's by a relative error of at most 0.0051.
Values may be sent and summed in bfloat16 or wider, within the bound.
A program may use at most 128 MiB of HBM per device.

```python
import jax
import jax.numpy as jnp
from jax import lax

D = 8192
SHORT = 7
LENGTH = 512


def block_scale(rng, extent, pieces, least, high):
    factor_of, own = 1.0, jax.random.fold_in(rng, 6)
    for position, shards_of in pieces:
        heights = jnp.exp(jax.random.uniform(jax.random.fold_in(own, position), (shards_of,), jnp.float32, least / len(pieces), high / len(pieces)))
        factor_of = factor_of * jnp.repeat(heights, extent[position] // shards_of).reshape([-1 if axis == position else 1 for axis in range(len(extent))])
    return factor_of


def scatter_about(key, extent, spread, most, pieces=(), held_as=jnp.bfloat16):
    level = block_scale(key, extent, pieces, -0.22, 0.18) if pieces else 1.0
    entries = jax.random.normal(key, extent, jnp.float32) * spread * level
    return jnp.minimum(jnp.maximum(entries, -most), most).astype(held_as)


def setup_inputs(seed: int = 0) -> dict:
    keys = jax.random.split(jax.random.key(seed), 6)
    return {
        "features": scatter_about(keys[0], (3, LENGTH, D), 1.0, 6.0, ((1, 4), (2, 8))),
        "short_kernel": scatter_about(keys[1], (3, SHORT, D), SHORT ** -0.5, 2.0, ((2, 8),), jnp.float32),
        "long_filter": scatter_about(keys[2], (LENGTH, D), LENGTH ** -0.5, 0.25, ((0, 4), (1, 8))),
        "out_weight": scatter_about(keys[3], (D, D), D ** -0.5, 0.0625, ((1, 8),)),
        "grad_out": scatter_about(keys[4], (LENGTH, D), 1.0, 6.0, ((0, 4), (1, 8))),
    }


def shift_down(values, steps):
    return jnp.pad(values, ((steps, 0), (0, 0)))[:values.shape[0]]


def shift_up(values, steps):
    return jnp.pad(values, ((0, steps), (0, 0)))[steps:]


def reference(features, short_kernel, long_filter, out_weight, grad_out):
    feats = features.astype(jnp.float32)
    length = feats.shape[1]
    convs = []
    for branch in range(3):
        total = jnp.zeros_like(feats[branch])
        for tap_index in range(SHORT):
            total = total + short_kernel[branch, tap_index] * shift_down(feats[branch], tap_index)
        convs.append(total)
    q_conv, k_conv, v_conv = convs
    gated = (k_conv * v_conv).astype(jnp.bfloat16)
    gated_wide = lax.optimization_barrier(gated).astype(jnp.float32)
    period = 2 * length
    filter_spec = jnp.fft.rfft(long_filter.astype(jnp.float32), n=period, axis=0)
    gated_spec = jnp.fft.rfft(gated_wide, n=period, axis=0)
    long_out = jnp.fft.irfft(filter_spec * gated_spec, n=period, axis=0)[:length]
    mixed = (q_conv * long_out).astype(jnp.bfloat16)
    grad_mixed = jnp.dot(grad_out, out_weight.T, preferred_element_type=jnp.float32)
    grad_long = (grad_mixed * q_conv).astype(jnp.bfloat16)
    grad_long_wide = lax.optimization_barrier(grad_long).astype(jnp.float32)
    grad_spec = jnp.fft.rfft(grad_long_wide, n=period, axis=0)
    grad_gated = jnp.fft.irfft(jnp.conj(filter_spec) * grad_spec, n=period, axis=0)[:length]
    grad_filter = jnp.fft.irfft(jnp.conj(gated_spec) * grad_spec, n=period, axis=0)[:length]
    grad_conv = [grad_mixed * long_out, grad_gated * v_conv, grad_gated * k_conv]
    feature_grads = []
    kernel_grads = []
    for branch in range(3):
        total = jnp.zeros_like(feats[branch])
        rows = []
        for tap_index in range(SHORT):
            total = total + short_kernel[branch, tap_index] * shift_up(grad_conv[branch], tap_index)
            rows.append(jnp.sum(grad_conv[branch] * shift_down(feats[branch], tap_index), axis=0))
        feature_grads.append(total.astype(jnp.bfloat16))
        kernel_grads.append(jnp.stack(rows, axis=0))
    grad_features = jnp.stack(feature_grads, axis=0)
    grad_kernel = jnp.stack(kernel_grads, axis=0)
    grad_weight = jnp.dot(mixed.T, grad_out, preferred_element_type=jnp.float32)
    return grad_features, grad_kernel, grad_filter, grad_weight
```

```python
import numpy as np

import jax
import jax.numpy as jnp
from jax import lax
from jax.sharding import PartitionSpec as P

BF16 = jnp.bfloat16
F32 = jnp.float32


def fourier_tables(length):
    period = 2 * length
    freq = np.arange(length)
    angles = (freq[:, None] * np.arange(length)[None, :] % period) * (2 * np.pi / period)
    cos_part, sin_part = np.cos(angles), -np.sin(angles)
    sin_part[0] = 1 - 2 * (np.arange(length) % 2)
    ahead = np.concatenate([cos_part, sin_part], axis=0)
    weight = np.full((length, 1), 2.0 / period)
    weight[0] = 1.0 / period
    back = np.concatenate([cos_part * weight, sin_part * weight], axis=0).T

    def halves(table):
        high = table.astype(np.float32).astype(BF16)
        low = (table - high.astype(np.float64)).astype(np.float32).astype(BF16)
        return high, low

    return halves(ahead) + halves(back)


def to_spectrum(high, low, block):
    return jnp.dot(high, block, preferred_element_type=F32) + jnp.dot(
        low, block, preferred_element_type=F32
    )


def from_spectrum(high, low, real_part, imag_part):
    half = real_part.shape[0]
    total = None
    for values, columns in ((real_part, slice(0, half)), (imag_part, slice(half, 2 * half))):
        upper = values.astype(BF16)
        rest = (values - upper.astype(F32)).astype(BF16)
        term = (
            jnp.dot(high[:, columns], upper, preferred_element_type=F32)
            + jnp.dot(low[:, columns], upper, preferred_element_type=F32)
            + jnp.dot(high[:, columns], rest, preferred_element_type=F32)
        )
        total = term if total is None else total + term
    return total


def spectral_product(first, second, conjugate):
    half = first.shape[0] // 2
    first_real, first_imag = first[:half], first[half:]
    second_real, second_imag = second[:half], second[half:]
    edge = lax.broadcasted_iota(jnp.int32, first_real.shape, 0) == 0
    real_real = first_real * second_real
    imag_imag = first_imag * second_imag
    if conjugate:
        real_part = real_real + imag_imag
        imag_part = first_real * second_imag - first_imag * second_real
    else:
        real_part = real_real - imag_imag
        imag_part = first_real * second_imag + first_imag * second_real
    return jnp.where(edge, real_real, real_part), jnp.where(edge, imag_imag, imag_part)


def shifted(array, axis, by):
    peers = lax.axis_size(axis)
    pairs = [(i, i + by) for i in range(peers) if 0 <= i + by < peers]
    return lax.ppermute(array, axis, pairs)


def whole_sequence(block):
    return lax.all_to_all(block, "ctx", split_axis=1, concat_axis=0, tiled=True)


def own_tokens(block):
    return lax.all_to_all(block, "ctx", split_axis=0, concat_axis=1, tiled=True)


def plain(features, short_kernel, long_filter, out_weight, grad_out):
    block_len, chans = features.shape[1:]
    taps = short_kernel.shape[1]
    margin = taps - 1
    ahead_high, ahead_low, back_high, back_low = fourier_tables(block_len * lax.axis_size("ctx"))
    partial_mixed = jnp.einsum("tc,dc->td", grad_out, out_weight, preferred_element_type=F32)
    grad_mixed = lax.psum_scatter(partial_mixed, "ch", scatter_dimension=1, tiled=True)
    before = shifted(features[:, block_len - margin :, :], "ctx", 1)
    extended = jnp.concatenate([before, features], axis=1).astype(F32)
    conv = jnp.zeros((3, block_len, chans), F32)
    for tap_index in range(taps):
        conv = (
            conv
            + short_kernel[:, tap_index, None, :]
            * extended[:, margin - tap_index : margin - tap_index + block_len, :]
        )
    q_conv, k_conv, v_conv = (conv[0], conv[1], conv[2])
    gated = (k_conv * v_conv).astype(BF16)
    filter_spec = to_spectrum(ahead_high, ahead_low, whole_sequence(long_filter))
    gated_spec = to_spectrum(ahead_high, ahead_low, whole_sequence(gated))
    out_spec = spectral_product(filter_spec, gated_spec, False)
    long_out = own_tokens(from_spectrum(back_high, back_low, *out_spec))
    mixed = (q_conv * long_out).astype(BF16)
    grad_long = (grad_mixed * q_conv).astype(BF16)
    grad_spec = to_spectrum(ahead_high, ahead_low, whole_sequence(grad_long))
    back_spec = spectral_product(filter_spec, grad_spec, True)
    grad_gated = own_tokens(from_spectrum(back_high, back_low, *back_spec))
    lag_spec = spectral_product(gated_spec, grad_spec, True)
    grad_filter = own_tokens(from_spectrum(back_high, back_low, *lag_spec))
    grad_conv = jnp.stack([grad_mixed * long_out, grad_gated * v_conv, grad_gated * k_conv], axis=0)
    after = shifted(grad_conv[:, :margin, :], "ctx", -1)
    grad_extended = jnp.concatenate([grad_conv, after], axis=1)
    feature_total = jnp.zeros((3, block_len, chans), F32)
    kernel_rows = []
    for tap_index in range(taps):
        feature_total = (
            feature_total
            + short_kernel[:, tap_index, None, :]
            * grad_extended[:, tap_index : tap_index + block_len, :]
        )
        kernel_rows.append(
            jnp.sum(
                grad_conv * extended[:, margin - tap_index : margin - tap_index + block_len, :],
                axis=1,
            )
        )
    grad_features = feature_total.astype(BF16)
    grad_kernel = lax.psum(jnp.stack(kernel_rows, axis=1), "ctx")
    all_mixed = whole_sequence(lax.all_gather(mixed, "ch", axis=1, tiled=True))
    all_grad_out = lax.all_gather(grad_out, "ctx", axis=0, tiled=True)
    grad_weight = jnp.einsum("tn,tc->nc", all_mixed, all_grad_out, preferred_element_type=F32)
    return (grad_features, grad_kernel, grad_filter, grad_weight)


def solution(mesh):
    return jax.shard_map(
        plain,
        mesh=mesh,
        in_specs=(
            P(None, "ctx", "ch"),
            P(None, None, "ch"),
            P("ctx", "ch"),
            P(None, "ch"),
            P("ctx", "ch"),
        ),
        out_specs=(P(None, "ctx", "ch"), P(None, None, "ch"), P("ctx", "ch"), P("ctx", "ch")),
        check_vma=False,
    )
```

```python
import numpy as np

import jax
import jax.numpy as jnp
from jax import lax
from jax.experimental import pallas as pl
from jax.experimental.pallas import tpu as pltpu
from jax.sharding import PartitionSpec as P

BF16 = jnp.bfloat16
F32 = jnp.float32


def fourier_tables(length):
    period = 2 * length
    freq = np.arange(length)
    angles = (freq[:, None] * np.arange(length)[None, :] % period) * (2 * np.pi / period)
    cos_part, sin_part = np.cos(angles), -np.sin(angles)
    sin_part[0] = 1 - 2 * (np.arange(length) % 2)
    ahead = np.concatenate([cos_part, sin_part], axis=0)
    weight = np.full((length, 1), 2.0 / period)
    weight[0] = 1.0 / period
    back = np.concatenate([cos_part * weight, sin_part * weight], axis=0).T

    def halves(table):
        high = table.astype(np.float32).astype(BF16)
        low = (table - high.astype(np.float64)).astype(np.float32).astype(BF16)
        return high, low

    return halves(ahead) + halves(back)


def to_spectrum(high, low, block):
    return jnp.dot(high, block, preferred_element_type=F32) + jnp.dot(
        low, block, preferred_element_type=F32
    )


def from_spectrum(high, low, real_part, imag_part):
    half = real_part.shape[0]
    total = None
    for values, columns in ((real_part, slice(0, half)), (imag_part, slice(half, 2 * half))):
        upper = values.astype(BF16)
        rest = (values - upper.astype(F32)).astype(BF16)
        term = (
            jnp.dot(high[:, columns], upper, preferred_element_type=F32)
            + jnp.dot(low[:, columns], upper, preferred_element_type=F32)
            + jnp.dot(high[:, columns], rest, preferred_element_type=F32)
        )
        total = term if total is None else total + term
    return total


def spectral_product(first, second, conjugate):
    half = first.shape[0] // 2
    first_real, first_imag = first[:half], first[half:]
    second_real, second_imag = second[:half], second[half:]
    edge = lax.broadcasted_iota(jnp.int32, first_real.shape, 0) == 0
    real_real = first_real * second_real
    imag_imag = first_imag * second_imag
    if conjugate:
        real_part = real_real + imag_imag
        imag_part = first_real * second_imag - first_imag * second_real
    else:
        real_part = real_real - imag_imag
        imag_part = first_real * second_imag + first_imag * second_real
    return jnp.where(edge, real_real, real_part), jnp.where(edge, imag_imag, imag_part)


def shifted(array, axis, by):
    peers = lax.axis_size(axis)
    pairs = [(i, i + by) for i in range(peers) if 0 <= i + by < peers]
    return lax.ppermute(array, axis, pairs)


def whole_sequence(block):
    return lax.all_to_all(block, "ctx", split_axis=1, concat_axis=0, tiled=True)


def own_tokens(block):
    return lax.all_to_all(block, "ctx", split_axis=0, concat_axis=1, tiled=True)


def plain(features, short_kernel, long_filter, out_weight, grad_out):
    block_len, chans = features.shape[1:]
    taps = short_kernel.shape[1]
    margin = taps - 1
    ahead_high, ahead_low, back_high, back_low = fourier_tables(block_len * lax.axis_size("ctx"))
    partial_mixed = jnp.einsum("tc,dc->td", grad_out, out_weight, preferred_element_type=F32)
    grad_mixed = lax.psum_scatter(partial_mixed, "ch", scatter_dimension=1, tiled=True)
    before = shifted(features[:, block_len - margin :, :], "ctx", 1)
    extended = jnp.concatenate([before, features], axis=1).astype(F32)
    conv = jnp.zeros((3, block_len, chans), F32)
    for tap_index in range(taps):
        conv = (
            conv
            + short_kernel[:, tap_index, None, :]
            * extended[:, margin - tap_index : margin - tap_index + block_len, :]
        )
    q_conv, k_conv, v_conv = (conv[0], conv[1], conv[2])
    gated = (k_conv * v_conv).astype(BF16)
    filter_spec = to_spectrum(ahead_high, ahead_low, whole_sequence(long_filter))
    gated_spec = to_spectrum(ahead_high, ahead_low, whole_sequence(gated))
    out_spec = spectral_product(filter_spec, gated_spec, False)
    long_out = own_tokens(from_spectrum(back_high, back_low, *out_spec))
    mixed = (q_conv * long_out).astype(BF16)
    grad_long = (grad_mixed * q_conv).astype(BF16)
    grad_spec = to_spectrum(ahead_high, ahead_low, whole_sequence(grad_long))
    back_spec = spectral_product(filter_spec, grad_spec, True)
    grad_gated = own_tokens(from_spectrum(back_high, back_low, *back_spec))
    lag_spec = spectral_product(gated_spec, grad_spec, True)
    grad_filter = own_tokens(from_spectrum(back_high, back_low, *lag_spec))
    grad_conv = jnp.stack([grad_mixed * long_out, grad_gated * v_conv, grad_gated * k_conv], axis=0)
    after = shifted(grad_conv[:, :margin, :], "ctx", -1)
    grad_extended = jnp.concatenate([grad_conv, after], axis=1)
    feature_total = jnp.zeros((3, block_len, chans), F32)
    kernel_rows = []
    for tap_index in range(taps):
        feature_total = (
            feature_total
            + short_kernel[:, tap_index, None, :]
            * grad_extended[:, tap_index : tap_index + block_len, :]
        )
        kernel_rows.append(
            jnp.sum(
                grad_conv * extended[:, margin - tap_index : margin - tap_index + block_len, :],
                axis=1,
            )
        )
    grad_features = feature_total.astype(BF16)
    grad_kernel = lax.psum(jnp.stack(kernel_rows, axis=1), "ctx")
    all_mixed = whole_sequence(lax.all_gather(mixed, "ch", axis=1, tiled=True))
    all_grad_out = lax.all_gather(grad_out, "ctx", axis=0, tiled=True)
    grad_weight = jnp.einsum("tn,tc->nc", all_mixed, all_grad_out, preferred_element_type=F32)
    return (grad_features, grad_kernel, grad_filter, grad_weight)


MESH = pl.DeviceIdType.MESH
EDGE = 16
NEXT_EDGE = 8
TILE = 128
ROWS = 256
W_SLOTS = 3


def fused_kernel(
    features,
    short_kernel,
    long_filter,
    out_weight,
    grad_out,
    ahead_high,
    ahead_low,
    back_high,
    back_low,
    grad_features,
    grad_kernel,
    grad_filter,
    all_grad_out,
    all_mixed,
    w_buf,
    pair_out,
    pair_in,
    partials,
    line_out,
    line_in,
    edge_in,
    extended,
    conv,
    filter_out,
    gated_out,
    grad_long_out,
    filter_wide,
    gated_wide,
    grad_wide,
    filter_spec,
    gated_spec,
    grad_spec,
    prod_high,
    prod_low,
    long_send,
    long_recv,
    back_send,
    back_recv,
    lag_send,
    lag_recv,
    mixed,
    grad_mixed,
    grad_conv,
    next_edge_in,
    kernel_parts,
    w_sem,
    local_sem,
    pair_sems,
    line_sems,
    edge_sems,
    next_sems,
    exchange_sems,
    mixed_sems,
    forward_sems,
):
    me_ctx, me_ch = lax.axis_index("ctx"), lax.axis_index("ch")
    n_ctx, lines = lax.axis_size("ctx"), lax.axis_size("ch") // 2
    core, z = lax.rem(me_ch, 2), me_ch // 2
    block_len, chans = grad_out.shape
    taps = short_kernel.shape[1]
    part = chans // n_ctx
    length = n_ctx * block_len
    hops = [k % lines for k in range(1, lines + 1)]

    def column(index):
        return pl.ds(pl.multiple_of(index * TILE, TILE), TILE)

    def token_rows(index):
        return pl.ds(pl.multiple_of(index * block_len, block_len), block_len)

    def remote(src, dst, sems, index, ctx, ch):
        return pltpu.make_async_remote_copy(
            src_ref=src,
            dst_ref=dst,
            send_sem=sems.at[0, index],
            recv_sem=sems.at[1, index],
            device_id={"ctx": ctx, "ch": ch},
            device_id_type=MESH,
        )

    weight_steps = []
    for k in hops:
        target = lax.rem(z + k, lines) * 2
        weight_steps += [target + 1 - core, target + core]

    def weight_copy(step):
        slot = step % W_SLOTS
        start = pl.multiple_of(weight_steps[step] * chans, chans)
        return pltpu.make_async_copy(
            out_weight.at[pl.ds(start, chans), :], w_buf.at[slot], w_sem.at[slot]
        )

    for step in range(W_SLOTS):
        weight_copy(step).start()

    barrier = pltpu.get_barrier_semaphore()
    group = me_ctx * lines + z
    for distance in range(1, n_ctx * lines):
        other = lax.rem(group + distance, n_ctx * lines)
        pl.semaphore_signal(
            barrier,
            inc=1,
            device_id={"ctx": other // lines, "ch": lax.rem(other, lines) * 2 + core},
            device_id_type=MESH,
        )
    pl.semaphore_signal(
        barrier, inc=1, device_id={"ctx": me_ctx, "ch": z * 2 + 1 - core}, device_id_type=MESH
    )

    def stage_filter(tile, carry):
        per_part = part // TILE
        filter_out[tile // per_part, :, column(lax.rem(tile, per_part))] = long_filter[
            :, column(tile)
        ]
        return carry

    lax.fori_loop(0, chans // TILE, stage_filter, 0)
    filter_wide[token_rows(me_ctx), :] = filter_out[me_ctx]
    pl.semaphore_wait(barrier, n_ctx * lines)

    def exchange(number, src_at, dst):
        copies = []
        for distance in range(1, n_ctx):
            peer = lax.rem(me_ctx + distance, n_ctx)
            copies.append(
                remote(
                    src_at(peer),
                    dst,
                    exchange_sems.at[number],
                    distance - 1,
                    peer,
                    me_ch,
                )
            )
        for copy in copies:
            copy.start()
        return copies

    def arrived(copies):
        for copy in copies:
            copy.wait_recv()

    edge_copy = remote(
        features.at[:, pl.ds(block_len - EDGE, EDGE), :],
        edge_in,
        edge_sems,
        0,
        lax.rem(me_ctx + 1, n_ctx),
        me_ch,
    )
    edge_copy.start()
    filter_copies = exchange(0, lambda peer: filter_out.at[peer], filter_wide.at[token_rows(me_ctx)])

    pair_copies, line_copies = [], []

    def finish_hop(index):
        pair_copies[index].wait_recv()
        if hops[index] == 0:
            partials[index] = partials[index] + pair_in[index].astype(F32)
            return
        line_out[index] = (partials[index] + pair_in[index].astype(F32)).astype(BF16)
        copy = remote(
            line_out.at[index],
            line_in.at[index],
            line_sems,
            index,
            me_ctx,
            lax.rem(z + hops[index], lines) * 2 + core,
        )
        copy.start()
        line_copies.append(copy)

    for step in range(2 * lines):
        index = step // 2
        slot = step % W_SLOTS
        weight_copy(step).wait()

        def project(tile, carry, step=step, index=index, slot=slot):
            rows = pl.ds(pl.multiple_of(tile * ROWS, ROWS), ROWS)
            value = lax.dot_general(
                grad_out[...],
                w_buf[slot, rows, :],
                (((1,), (1,)), ((), ())),
                preferred_element_type=F32,
            )
            if step % 2 == 0:
                pair_out[index, :, rows] = value.astype(BF16)
            else:
                partials[index, :, rows] = value
            return carry

        lax.fori_loop(0, chans // ROWS, project, 0)
        if step + W_SLOTS < 2 * lines:
            weight_copy(step + W_SLOTS).start()
        if step % 2 == 0:
            copy = remote(
                pair_out.at[index], pair_in.at[index], pair_sems, index, me_ctx, z * 2 + 1 - core
            )
            copy.start()
            pair_copies.append(copy)
            if index >= 1:
                finish_hop(index - 1)

    edge_copy.wait_recv()

    def convolve(tile, carry):
        cols = column(tile)
        totals = []
        for branch in range(3):
            edge = edge_in[branch, :, cols].astype(F32)
            extended[branch, 0:EDGE, cols] = jnp.where(me_ctx > 0, edge, 0.0)
            extended[branch, EDGE : EDGE + block_len, cols] = features[branch, :, cols].astype(F32)
            total = None
            for tap in range(taps):
                term = (
                    short_kernel[branch, tap : tap + 1, cols]
                    * extended[branch, EDGE - tap : EDGE - tap + block_len, cols]
                )
                total = term if total is None else total + term
            conv[branch, :, cols] = total
            totals.append(total)
        per_part = part // TILE
        gated_out[tile // per_part, :, column(lax.rem(tile, per_part))] = (
            totals[1] * totals[2]
        ).astype(BF16)
        return carry

    lax.fori_loop(0, chans // TILE, convolve, 0)
    gated_copies = exchange(1, lambda peer: gated_out.at[peer], gated_wide.at[token_rows(me_ctx)])
    gated_wide[token_rows(me_ctx), :] = gated_out[me_ctx]
    finish_hop(lines - 1)
    own_grad_out = pltpu.make_async_copy(grad_out, all_grad_out.at[me_ctx], local_sem.at[0])
    own_grad_out.start()

    def transform(source, target):
        def body(tile, carry):
            rows = pl.ds(pl.multiple_of(tile * ROWS, ROWS), ROWS)
            target[rows, :] = to_spectrum(ahead_high[rows, :], ahead_low[rows, :], source[...])
            return carry

        lax.fori_loop(0, 2 * length // ROWS, body, 0)

    def multiply(first, second, conjugate):
        step_rows = 32

        def body(tile, carry):
            upper = pl.ds(pl.multiple_of(tile * step_rows, step_rows), step_rows)
            lower = pl.ds(pl.multiple_of(length + tile * step_rows, step_rows), step_rows)
            first_real, first_imag = first[upper, :], first[lower, :]
            second_real, second_imag = second[upper, :], second[lower, :]
            row = lax.broadcasted_iota(jnp.int32, first_real.shape, 0) + tile * step_rows
            edge = row == 0
            real_real = first_real * second_real
            imag_imag = first_imag * second_imag
            if conjugate:
                real_part = real_real + imag_imag
                imag_part = first_real * second_imag - first_imag * second_real
            else:
                real_part = real_real - imag_imag
                imag_part = first_real * second_imag + first_imag * second_real
            for rows, value in (
                (upper, jnp.where(edge, real_real, real_part)),
                (lower, jnp.where(edge, imag_imag, imag_part)),
            ):
                high = value.astype(BF16)
                prod_high[rows, :] = high
                prod_low[rows, :] = (value - high.astype(F32)).astype(BF16)
            return carry

        lax.fori_loop(0, length // step_rows, body, 0)

    def invert(target):
        def body(tile, carry):
            rows = token_rows(tile)
            high, low = back_high[rows, :], back_low[rows, :]
            target[tile] = (
                jnp.dot(high, prod_high[...], preferred_element_type=F32)
                + jnp.dot(low, prod_high[...], preferred_element_type=F32)
                + jnp.dot(high, prod_low[...], preferred_element_type=F32)
            ).astype(BF16)
            return carry

        lax.fori_loop(0, n_ctx, body, 0)

    arrived(filter_copies)
    transform(filter_wide, filter_spec)
    arrived(gated_copies)
    transform(gated_wide, gated_spec)
    multiply(filter_spec, gated_spec, False)
    invert(long_send)
    long_copies = exchange(2, lambda peer: long_send.at[peer], long_recv.at[me_ctx])
    long_recv[me_ctx] = long_send[me_ctx]
    grad_out_copies = exchange(3, lambda peer: grad_out, all_grad_out.at[me_ctx])

    arrived(long_copies)

    def per_part_view(ref, tile):
        per_part = part // TILE
        return ref[tile // per_part, :, column(lax.rem(tile, per_part))].astype(F32)

    def mix(tile, carry):
        cols = column(tile)
        mixed[:, cols] = (conv[0, :, cols] * per_part_view(long_recv, tile)).astype(BF16)
        return carry

    lax.fori_loop(0, chans // TILE, mix, 0)

    def mixed_copy(k):
        return pltpu.make_async_remote_copy(
            src_ref=mixed,
            dst_ref=all_mixed.at[core, me_ctx],
            send_sem=mixed_sems.at[0, k],
            recv_sem=mixed_sems.at[1, me_ctx],
            device_id={"ctx": z, "ch": lax.rem(z + k, lines) * 2 + core},
            device_id_type=MESH,
        )

    own_mixed = pltpu.make_async_copy(mixed, all_mixed.at[core, me_ctx], local_sem.at[1])
    mine = me_ctx == z
    for k in range(1, lines):
        mixed_copy(k).start()

    @pl.when(mine)
    def _():
        own_mixed.start()

    @pl.when(jnp.logical_not(mine))
    def _():
        mixed_copy(0).start()

    for copy in line_copies:
        copy.wait_recv()

    def take_grad(tile, carry):
        cols = column(tile)
        total = partials[lines - 1, :, cols]
        for index in range(lines - 1):
            total = total + line_in[index, :, cols].astype(F32)
        grad_mixed[:, cols] = total
        per_part = part // TILE
        grad_long_out[tile // per_part, :, column(lax.rem(tile, per_part))] = (
            total * conv[0, :, cols]
        ).astype(BF16)
        return carry

    lax.fori_loop(0, chans // TILE, take_grad, 0)
    grad_copies = exchange(
        4, lambda peer: grad_long_out.at[peer], grad_wide.at[token_rows(me_ctx)]
    )
    grad_wide[token_rows(me_ctx), :] = grad_long_out[me_ctx]
    arrived(grad_copies)
    transform(grad_wide, grad_spec)
    multiply(filter_spec, grad_spec, True)
    invert(back_send)
    back_copies = exchange(5, lambda peer: back_send.at[peer], back_recv.at[me_ctx])
    back_recv[me_ctx] = back_send[me_ctx]
    multiply(gated_spec, grad_spec, True)
    invert(lag_send)
    lag_copies = exchange(6, lambda peer: lag_send.at[peer], lag_recv.at[me_ctx])
    lag_recv[me_ctx] = lag_send[me_ctx]
    arrived(back_copies)

    def conv_gradient(tile, carry):
        cols = column(tile)
        back = per_part_view(back_recv, tile)
        grad_conv[0, 0:block_len, cols] = grad_mixed[:, cols] * per_part_view(long_recv, tile)
        grad_conv[1, 0:block_len, cols] = back * conv[2, :, cols]
        grad_conv[2, 0:block_len, cols] = back * conv[1, :, cols]
        return carry

    lax.fori_loop(0, chans // TILE, conv_gradient, 0)
    next_copy = remote(
        grad_conv.at[:, pl.ds(0, NEXT_EDGE), :],
        next_edge_in,
        next_sems,
        0,
        lax.rem(me_ctx + n_ctx - 1, n_ctx),
        me_ch,
    )
    next_copy.start()

    def tap_gradient(tile, carry):
        cols = column(tile)
        for branch in range(3):
            values = grad_conv[branch, 0:block_len, cols]
            for tap in range(taps):
                term = values * extended[branch, EDGE - tap : EDGE - tap + block_len, cols]
                kernel_parts[me_ctx, branch, tap : tap + 1, cols] = jnp.sum(
                    term, axis=0, keepdims=True
                )
            kernel_parts[me_ctx, branch, taps : taps + 1, cols] = jnp.zeros((1, TILE), F32)
        return carry

    lax.fori_loop(0, chans // TILE, tap_gradient, 0)
    kernel_copies = exchange(7, lambda peer: kernel_parts.at[me_ctx], kernel_parts.at[me_ctx])
    next_copy.wait()

    def feature_gradient(tile, carry):
        cols = column(tile)
        for branch in range(3):
            grad_conv[branch, block_len : block_len + NEXT_EDGE, cols] = jnp.where(
                me_ctx < n_ctx - 1, next_edge_in[branch, :, cols], 0.0
            )
            total = None
            for tap in range(taps):
                term = (
                    short_kernel[branch, tap : tap + 1, cols]
                    * grad_conv[branch, tap : tap + block_len, cols]
                )
                total = term if total is None else total + term
            grad_features[branch, :, cols] = total.astype(BF16)
        return carry

    lax.fori_loop(0, chans // TILE, feature_gradient, 0)

    forward_copies = []
    for source in range(n_ctx):
        here = jnp.logical_and(mine, me_ctx == source)

        @pl.when(here)
        def _():
            own_mixed.wait()

        @pl.when(jnp.logical_not(here))
        def _(source=source):
            slot = all_mixed.at[core, source]
            remote(mixed, slot, mixed_sems, source, me_ctx, z * 2 + 1 - core).wait_recv()

        copy = remote(
            all_mixed.at[core, source],
            all_mixed.at[core, source],
            forward_sems,
            source,
            me_ctx,
            z * 2 + 1 - core,
        )
        copy.start()
        forward_copies.append(copy)

    arrived(lag_copies)

    def filter_gradient(tile, carry):
        grad_filter[:, column(tile)] = per_part_view(lag_recv, tile)
        return carry

    lax.fori_loop(0, chans // TILE, filter_gradient, 0)
    arrived(kernel_copies)
    total = kernel_parts[0]
    for index in range(1, n_ctx):
        total = total + kernel_parts[index]
    grad_kernel[...] = total[:, :taps, :]
    arrived(grad_out_copies)
    own_grad_out.wait()
    for copy in forward_copies:
        copy.wait()
    edge_copy.wait_send()
    for copies in (
        filter_copies,
        gated_copies,
        long_copies,
        grad_out_copies,
        grad_copies,
        back_copies,
        lag_copies,
        kernel_copies,
        pair_copies,
        line_copies,
    ):
        for copy in copies:
            copy.wait_send()
    for k in range(1, lines):
        mixed_copy(k).wait_send()

    @pl.when(jnp.logical_not(mine))
    def _():
        mixed_copy(0).wait_send()


def fused(features, short_kernel, long_filter, out_weight, grad_out):
    block_len, chans = grad_out.shape
    taps = short_kernel.shape[1]
    n_ctx, lines = lax.axis_size("ctx"), lax.axis_size("ch") // 2
    part, length = chans // n_ctx, n_ctx * block_len
    tables = [jnp.asarray(table) for table in fourier_tables(length)]
    in_vmem = pl.BlockSpec(memory_space=pltpu.VMEM)
    in_place = pl.BlockSpec(memory_space=pl.ANY)
    staged = pltpu.VMEM((n_ctx, block_len, part), BF16)
    wide = pltpu.VMEM((length, part), BF16)
    spectra = pltpu.VMEM((2 * length, part), F32)
    blocks = pltpu.VMEM((lines, block_len, chans), BF16)
    scratch = [
        pltpu.VMEM((W_SLOTS, chans, chans), BF16),
        blocks,
        blocks,
        pltpu.VMEM((lines, block_len, chans), F32),
        blocks,
        blocks,
        pltpu.VMEM((3, EDGE, chans), BF16),
        pltpu.VMEM((3, EDGE + block_len, chans), F32),
        pltpu.VMEM((3, block_len, chans), F32),
        staged,
        staged,
        staged,
        wide,
        wide,
        wide,
        spectra,
        spectra,
        spectra,
        pltpu.VMEM((2 * length, part), BF16),
        pltpu.VMEM((2 * length, part), BF16),
        staged,
        staged,
        staged,
        staged,
        staged,
        staged,
        pltpu.VMEM((block_len, chans), BF16),
        pltpu.VMEM((block_len, chans), F32),
        pltpu.VMEM((3, block_len + NEXT_EDGE, chans), F32),
        pltpu.VMEM((3, NEXT_EDGE, chans), F32),
        pltpu.VMEM((n_ctx, 3, taps + 1, chans), F32),
        pltpu.SemaphoreType.DMA((W_SLOTS,)),
        pltpu.SemaphoreType.DMA((2,)),
        pltpu.SemaphoreType.DMA((2, lines)),
        pltpu.SemaphoreType.DMA((2, lines)),
        pltpu.SemaphoreType.DMA((2, 1)),
        pltpu.SemaphoreType.DMA((2, 1)),
        pltpu.SemaphoreType.DMA((8, 2, n_ctx - 1)),
        pltpu.SemaphoreType.DMA((2, max(lines, n_ctx))),
        pltpu.SemaphoreType.DMA((2, n_ctx)),
    ]
    grad_features, grad_kernel, grad_filter, all_grad_out, all_mixed = pl.pallas_call(
        fused_kernel,
        out_shape=[
            jax.ShapeDtypeStruct(features.shape, BF16),
            jax.ShapeDtypeStruct(short_kernel.shape, F32),
            jax.ShapeDtypeStruct(long_filter.shape, F32),
            jax.ShapeDtypeStruct((n_ctx, block_len, chans), BF16),
            jax.ShapeDtypeStruct((2, n_ctx, block_len, chans), BF16),
        ],
        in_specs=[in_vmem, in_vmem, in_vmem, in_place] + [in_vmem] * 5,
        out_specs=[in_vmem, in_vmem, in_vmem, in_place, in_place],
        scratch_shapes=scratch,
        compiler_params=pltpu.CompilerParams(
            collective_id=0, has_side_effects=True, vmem_limit_bytes=56 * 1024 * 1024
        ),
        cost_estimate=pl.CostEstimate(
            flops=8 * 10**9, bytes_accessed=28 * 2**20, transcendentals=0
        ),
    )(features, short_kernel, long_filter, out_weight, grad_out, *tables)
    grad_weight = jnp.einsum(
        "ktn,tc->knc",
        all_mixed.reshape(2, length, chans),
        all_grad_out.reshape(length, chans),
        preferred_element_type=F32,
    ).reshape(2 * chans, chans)
    return (grad_features, grad_kernel, grad_filter, grad_weight)


def solution(mesh):
    n_ctx, n_ch = mesh.shape["ctx"], mesh.shape["ch"]

    def local(features, short_kernel, long_filter, out_weight, grad_out):
        aligned = grad_out.shape[1] % (TILE * n_ctx) == 0 and grad_out.shape[1] % ROWS == 0
        body = fused if n_ch == 2 * n_ctx and aligned else plain
        return body(features, short_kernel, long_filter, out_weight, grad_out)

    return jax.shard_map(
        local,
        mesh=mesh,
        in_specs=(
            P(None, "ctx", "ch"),
            P(None, None, "ch"),
            P("ctx", "ch"),
            P(None, "ch"),
            P("ctx", "ch"),
        ),
        out_specs=(P(None, "ctx", "ch"), P(None, None, "ch"), P("ctx", "ch"), P("ctx", "ch")),
        check_vma=False,
    )
```

```python
import numpy as np

import jax
import jax.numpy as jnp
from jax import lax
from jax.experimental import pallas as pl
from jax.experimental.pallas import tpu as pltpu
from jax.sharding import PartitionSpec as P

BF16 = jnp.bfloat16
F32 = jnp.float32


def fourier_tables(length):
    period = 2 * length
    freq = np.arange(length)
    angles = (freq[:, None] * np.arange(length)[None, :] % period) * (2 * np.pi / period)
    cos_part, sin_part = np.cos(angles), -np.sin(angles)
    sin_part[0] = 1 - 2 * (np.arange(length) % 2)
    ahead = np.concatenate([cos_part, sin_part], axis=0)
    weight = np.full((length, 1), 2.0 / period)
    weight[0] = 1.0 / period
    back = np.concatenate([cos_part * weight, sin_part * weight], axis=0).T

    def halves(table):
        high = table.astype(np.float32).astype(BF16)
        low = (table - high.astype(np.float64)).astype(np.float32).astype(BF16)
        return high, low

    return halves(ahead) + halves(back)


def to_spectrum(high, low, block):
    return jnp.dot(high, block, preferred_element_type=F32) + jnp.dot(
        low, block, preferred_element_type=F32
    )


def from_spectrum(high, low, real_part, imag_part):
    half = real_part.shape[0]
    total = None
    for values, columns in ((real_part, slice(0, half)), (imag_part, slice(half, 2 * half))):
        upper = values.astype(BF16)
        rest = (values - upper.astype(F32)).astype(BF16)
        term = (
            jnp.dot(high[:, columns], upper, preferred_element_type=F32)
            + jnp.dot(low[:, columns], upper, preferred_element_type=F32)
            + jnp.dot(high[:, columns], rest, preferred_element_type=F32)
        )
        total = term if total is None else total + term
    return total


def spectral_product(first, second, conjugate):
    half = first.shape[0] // 2
    first_real, first_imag = first[:half], first[half:]
    second_real, second_imag = second[:half], second[half:]
    edge = lax.broadcasted_iota(jnp.int32, first_real.shape, 0) == 0
    real_real = first_real * second_real
    imag_imag = first_imag * second_imag
    if conjugate:
        real_part = real_real + imag_imag
        imag_part = first_real * second_imag - first_imag * second_real
    else:
        real_part = real_real - imag_imag
        imag_part = first_real * second_imag + first_imag * second_real
    return jnp.where(edge, real_real, real_part), jnp.where(edge, imag_imag, imag_part)


def shifted(array, axis, by):
    peers = lax.axis_size(axis)
    pairs = [(i, i + by) for i in range(peers) if 0 <= i + by < peers]
    return lax.ppermute(array, axis, pairs)


def whole_sequence(block):
    return lax.all_to_all(block, "ctx", split_axis=1, concat_axis=0, tiled=True)


def own_tokens(block):
    return lax.all_to_all(block, "ctx", split_axis=0, concat_axis=1, tiled=True)


def plain(features, short_kernel, long_filter, out_weight, grad_out):
    block_len, chans = features.shape[1:]
    taps = short_kernel.shape[1]
    margin = taps - 1
    ahead_high, ahead_low, back_high, back_low = fourier_tables(block_len * lax.axis_size("ctx"))
    partial_mixed = jnp.einsum("tc,dc->td", grad_out, out_weight, preferred_element_type=F32)
    grad_mixed = lax.psum_scatter(partial_mixed, "ch", scatter_dimension=1, tiled=True)
    before = shifted(features[:, block_len - margin :, :], "ctx", 1)
    extended = jnp.concatenate([before, features], axis=1).astype(F32)
    conv = jnp.zeros((3, block_len, chans), F32)
    for tap_index in range(taps):
        conv = (
            conv
            + short_kernel[:, tap_index, None, :]
            * extended[:, margin - tap_index : margin - tap_index + block_len, :]
        )
    q_conv, k_conv, v_conv = (conv[0], conv[1], conv[2])
    gated = (k_conv * v_conv).astype(BF16)
    filter_spec = to_spectrum(ahead_high, ahead_low, whole_sequence(long_filter))
    gated_spec = to_spectrum(ahead_high, ahead_low, whole_sequence(gated))
    out_spec = spectral_product(filter_spec, gated_spec, False)
    long_out = own_tokens(from_spectrum(back_high, back_low, *out_spec))
    mixed = (q_conv * long_out).astype(BF16)
    grad_long = (grad_mixed * q_conv).astype(BF16)
    grad_spec = to_spectrum(ahead_high, ahead_low, whole_sequence(grad_long))
    back_spec = spectral_product(filter_spec, grad_spec, True)
    grad_gated = own_tokens(from_spectrum(back_high, back_low, *back_spec))
    lag_spec = spectral_product(gated_spec, grad_spec, True)
    grad_filter = own_tokens(from_spectrum(back_high, back_low, *lag_spec))
    grad_conv = jnp.stack([grad_mixed * long_out, grad_gated * v_conv, grad_gated * k_conv], axis=0)
    after = shifted(grad_conv[:, :margin, :], "ctx", -1)
    grad_extended = jnp.concatenate([grad_conv, after], axis=1)
    feature_total = jnp.zeros((3, block_len, chans), F32)
    kernel_rows = []
    for tap_index in range(taps):
        feature_total = (
            feature_total
            + short_kernel[:, tap_index, None, :]
            * grad_extended[:, tap_index : tap_index + block_len, :]
        )
        kernel_rows.append(
            jnp.sum(
                grad_conv * extended[:, margin - tap_index : margin - tap_index + block_len, :],
                axis=1,
            )
        )
    grad_features = feature_total.astype(BF16)
    grad_kernel = lax.psum(jnp.stack(kernel_rows, axis=1), "ctx")
    all_mixed = whole_sequence(lax.all_gather(mixed, "ch", axis=1, tiled=True))
    all_grad_out = lax.all_gather(grad_out, "ctx", axis=0, tiled=True)
    grad_weight = jnp.einsum("tn,tc->nc", all_mixed, all_grad_out, preferred_element_type=F32)
    return (grad_features, grad_kernel, grad_filter, grad_weight)


MESH = pl.DeviceIdType.MESH
EDGE = 16
NEXT_EDGE = 8
TILE = 128
ROWS = 256
W_SLOTS = 3


def fused_kernel(
    features,
    short_kernel,
    long_filter,
    out_weight,
    grad_out,
    ahead_high,
    ahead_low,
    back_high,
    back_low,
    grad_features,
    grad_kernel,
    grad_filter,
    all_grad_out,
    all_mixed,
    w_buf,
    pair_out,
    pair_in,
    partials,
    line_out,
    line_in,
    edge_in,
    extended,
    conv,
    filter_out,
    gated_out,
    grad_long_out,
    filter_wide,
    gated_wide,
    grad_wide,
    filter_spec,
    gated_spec,
    grad_spec,
    prod_high,
    prod_low,
    long_send,
    long_recv,
    back_send,
    back_recv,
    lag_send,
    lag_recv,
    line_mixed,
    grad_mixed,
    grad_conv,
    next_edge_in,
    kernel_parts,
    w_sem,
    local_sem,
    pair_sems,
    line_sems,
    edge_sems,
    next_sems,
    exchange_sems,
    chain_sems,
    relay_sems,
    forward_sems,
):
    me_ctx, me_ch = lax.axis_index("ctx"), lax.axis_index("ch")
    n_ctx, lines = lax.axis_size("ctx"), lax.axis_size("ch") // 2
    core, z = lax.rem(me_ch, 2), me_ch // 2
    block_len, chans = grad_out.shape
    taps = short_kernel.shape[1]
    part = chans // n_ctx
    length = n_ctx * block_len
    hops = [k % lines for k in range(1, lines + 1)]

    def column(index):
        return pl.ds(pl.multiple_of(index * TILE, TILE), TILE)

    def token_rows(index):
        return pl.ds(pl.multiple_of(index * block_len, block_len), block_len)

    def remote(src, dst, sems, index, ctx, ch):
        return pltpu.make_async_remote_copy(
            src_ref=src,
            dst_ref=dst,
            send_sem=sems.at[0, index],
            recv_sem=sems.at[1, index],
            device_id={"ctx": ctx, "ch": ch},
            device_id_type=MESH,
        )

    weight_steps = []
    for k in hops:
        target = lax.rem(z + k, lines) * 2
        weight_steps += [target + 1 - core, target + core]

    def weight_copy(step):
        slot = step % W_SLOTS
        start = pl.multiple_of(weight_steps[step] * chans, chans)
        return pltpu.make_async_copy(
            out_weight.at[pl.ds(start, chans), :], w_buf.at[slot], w_sem.at[slot]
        )

    for step in range(W_SLOTS):
        weight_copy(step).start()

    barrier = pltpu.get_barrier_semaphore()
    greeted = [(lax.rem(me_ctx + d, n_ctx), me_ch) for d in range(1, n_ctx)]
    greeted += [(me_ctx, lax.rem(z + d, lines) * 2 + core) for d in range(1, lines)]
    greeted.append((me_ctx, z * 2 + 1 - core))
    for ctx, ch in greeted:
        pl.semaphore_signal(
            barrier, inc=1, device_id={"ctx": ctx, "ch": ch}, device_id_type=MESH
        )

    def stage_filter(tile, carry):
        per_part = part // TILE
        filter_out[tile // per_part, :, column(lax.rem(tile, per_part))] = long_filter[
            :, column(tile)
        ]
        return carry

    lax.fori_loop(0, chans // TILE, stage_filter, 0)
    filter_wide[token_rows(me_ctx), :] = filter_out[me_ctx]
    pl.semaphore_wait(barrier, len(greeted))

    def exchange(number, src_at, dst):
        copies = []
        for distance in range(1, n_ctx):
            peer = lax.rem(me_ctx + distance, n_ctx)
            copies.append(
                remote(
                    src_at(peer),
                    dst,
                    exchange_sems.at[number],
                    distance - 1,
                    peer,
                    me_ch,
                )
            )
        for copy in copies:
            copy.start()
        return copies

    def arrived(copies):
        for copy in copies:
            copy.wait_recv()

    edge_copy = remote(
        features.at[:, pl.ds(block_len - EDGE, EDGE), :],
        edge_in,
        edge_sems,
        0,
        lax.rem(me_ctx + 1, n_ctx),
        me_ch,
    )
    edge_copy.start()
    filter_copies = exchange(0, lambda peer: filter_out.at[peer], filter_wide.at[token_rows(me_ctx)])

    pair_copies, line_copies = [], []

    def finish_hop(index):
        pair_copies[index].wait_recv()
        if hops[index] == 0:
            partials[index] = partials[index] + pair_in[index].astype(F32)
            return
        line_out[index] = (partials[index] + pair_in[index].astype(F32)).astype(BF16)
        copy = remote(
            line_out.at[index],
            line_in.at[index],
            line_sems,
            index,
            me_ctx,
            lax.rem(z + hops[index], lines) * 2 + core,
        )
        copy.start()
        line_copies.append(copy)

    for step in range(2 * lines):
        index = step // 2
        slot = step % W_SLOTS
        weight_copy(step).wait()

        def project(tile, carry, step=step, index=index, slot=slot):
            rows = pl.ds(pl.multiple_of(tile * ROWS, ROWS), ROWS)
            value = lax.dot_general(
                grad_out[...],
                w_buf[slot, rows, :],
                (((1,), (1,)), ((), ())),
                preferred_element_type=F32,
            )
            if step % 2 == 0:
                pair_out[index, :, rows] = value.astype(BF16)
            else:
                partials[index, :, rows] = value
            return carry

        lax.fori_loop(0, chans // ROWS, project, 0)
        if step + W_SLOTS < 2 * lines:
            weight_copy(step + W_SLOTS).start()
        if step % 2 == 0:
            copy = remote(
                pair_out.at[index], pair_in.at[index], pair_sems, index, me_ctx, z * 2 + 1 - core
            )
            copy.start()
            pair_copies.append(copy)
            if index >= 1:
                finish_hop(index - 1)

    edge_copy.wait_recv()

    def convolve(tile, carry):
        cols = column(tile)
        totals = []
        for branch in range(3):
            edge = edge_in[branch, :, cols].astype(F32)
            extended[branch, 0:EDGE, cols] = jnp.where(me_ctx > 0, edge, 0.0)
            extended[branch, EDGE : EDGE + block_len, cols] = features[branch, :, cols].astype(F32)
            total = None
            for tap in range(taps):
                term = (
                    short_kernel[branch, tap : tap + 1, cols]
                    * extended[branch, EDGE - tap : EDGE - tap + block_len, cols]
                )
                total = term if total is None else total + term
            conv[branch, :, cols] = total
            totals.append(total)
        per_part = part // TILE
        gated_out[tile // per_part, :, column(lax.rem(tile, per_part))] = (
            totals[1] * totals[2]
        ).astype(BF16)
        return carry

    lax.fori_loop(0, chans // TILE, convolve, 0)
    gated_copies = exchange(1, lambda peer: gated_out.at[peer], gated_wide.at[token_rows(me_ctx)])
    gated_wide[token_rows(me_ctx), :] = gated_out[me_ctx]
    finish_hop(lines - 1)
    own_grad_out = pltpu.make_async_copy(grad_out, all_grad_out.at[me_ctx], local_sem.at[0])
    own_grad_out.start()

    def transform(source, target):
        def body(tile, carry):
            rows = pl.ds(pl.multiple_of(tile * ROWS, ROWS), ROWS)
            target[rows, :] = to_spectrum(ahead_high[rows, :], ahead_low[rows, :], source[...])
            return carry

        lax.fori_loop(0, 2 * length // ROWS, body, 0)

    def multiply(first, second, conjugate):
        step_rows = 32

        def body(tile, carry):
            upper = pl.ds(pl.multiple_of(tile * step_rows, step_rows), step_rows)
            lower = pl.ds(pl.multiple_of(length + tile * step_rows, step_rows), step_rows)
            first_real, first_imag = first[upper, :], first[lower, :]
            second_real, second_imag = second[upper, :], second[lower, :]
            row = lax.broadcasted_iota(jnp.int32, first_real.shape, 0) + tile * step_rows
            edge = row == 0
            real_real = first_real * second_real
            imag_imag = first_imag * second_imag
            if conjugate:
                real_part = real_real + imag_imag
                imag_part = first_real * second_imag - first_imag * second_real
            else:
                real_part = real_real - imag_imag
                imag_part = first_real * second_imag + first_imag * second_real
            for rows, value in (
                (upper, jnp.where(edge, real_real, real_part)),
                (lower, jnp.where(edge, imag_imag, imag_part)),
            ):
                high = value.astype(BF16)
                prod_high[rows, :] = high
                prod_low[rows, :] = (value - high.astype(F32)).astype(BF16)
            return carry

        lax.fori_loop(0, length // step_rows, body, 0)

    def invert(target):
        def body(tile, carry):
            rows = token_rows(tile)
            high, low = back_high[rows, :], back_low[rows, :]
            target[tile] = (
                jnp.dot(high, prod_high[...], preferred_element_type=F32)
                + jnp.dot(low, prod_high[...], preferred_element_type=F32)
                + jnp.dot(high, prod_low[...], preferred_element_type=F32)
            ).astype(BF16)
            return carry

        lax.fori_loop(0, n_ctx, body, 0)

    arrived(filter_copies)
    transform(filter_wide, filter_spec)
    arrived(gated_copies)
    transform(gated_wide, gated_spec)
    multiply(filter_spec, gated_spec, False)
    invert(long_send)
    long_copies = exchange(2, lambda peer: long_send.at[peer], long_recv.at[me_ctx])
    long_recv[me_ctx] = long_send[me_ctx]
    grad_out_copies = exchange(3, lambda peer: grad_out, all_grad_out.at[me_ctx])

    arrived(long_copies)

    def per_part_view(ref, tile):
        per_part = part // TILE
        return ref[tile // per_part, :, column(lax.rem(tile, per_part))].astype(F32)

    def mix(tile, carry):
        cols = column(tile)
        line_mixed[z, :, cols] = (conv[0, :, cols] * per_part_view(long_recv, tile)).astype(BF16)
        return carry

    lax.fori_loop(0, chans // TILE, mix, 0)

    def chain_copy(sign, distance):
        block = line_mixed.at[z - sign * (distance - 1)]
        way = 0 if sign > 0 else 1
        return remote(
            block, block, chain_sems.at[way], distance - 1, me_ctx, (z + sign) * 2 + core
        )

    def chain_sends(sign, distance):
        first, after = z - sign * (distance - 1), z + sign
        inside = jnp.logical_and(first >= 0, first < lines)
        return jnp.logical_and(inside, jnp.logical_and(after >= 0, after < lines))

    def chain_receives(sign, distance):
        first = z - sign * distance
        return jnp.logical_and(first >= 0, first < lines)

    own_relay = pltpu.make_async_copy(
        line_mixed.at[me_ctx], all_mixed.at[core, me_ctx], local_sem.at[1]
    )

    def relay_copy(block):
        return pltpu.make_async_remote_copy(
            src_ref=line_mixed.at[block],
            dst_ref=all_mixed.at[core, me_ctx],
            send_sem=relay_sems.at[0, block],
            recv_sem=relay_sems.at[1, me_ctx],
            device_id={"ctx": block, "ch": me_ch},
            device_id_type=MESH,
        )

    def relay(block):
        @pl.when(block == me_ctx)
        def _():
            own_relay.start()

        @pl.when(block != me_ctx)
        def _():
            relay_copy(block).start()

    def chain_start(distance):
        for sign in (1, -1):

            @pl.when(chain_sends(sign, distance))
            def _(sign=sign):
                chain_copy(sign, distance).start()

    def chain_take(distance):
        for sign in (1, -1):

            @pl.when(chain_receives(sign, distance))
            def _(sign=sign):
                chain_copy(sign, distance).wait_recv()

        if distance + 1 < lines:
            chain_start(distance + 1)
        for sign in (1, -1):

            @pl.when(chain_receives(sign, distance))
            def _(sign=sign):
                relay(z - sign * distance)

    for copy in line_copies:
        copy.wait_recv()
    chain_start(1)
    relay(z)

    def take_grad(tile, carry):
        cols = column(tile)
        total = partials[lines - 1, :, cols]
        for index in range(lines - 1):
            total = total + line_in[index, :, cols].astype(F32)
        grad_mixed[:, cols] = total
        per_part = part // TILE
        grad_long_out[tile // per_part, :, column(lax.rem(tile, per_part))] = (
            total * conv[0, :, cols]
        ).astype(BF16)
        return carry

    lax.fori_loop(0, chans // TILE, take_grad, 0)
    grad_copies = exchange(
        4, lambda peer: grad_long_out.at[peer], grad_wide.at[token_rows(me_ctx)]
    )
    grad_wide[token_rows(me_ctx), :] = grad_long_out[me_ctx]
    arrived(grad_copies)
    transform(grad_wide, grad_spec)
    chain_take(1)
    multiply(filter_spec, grad_spec, True)
    invert(back_send)
    back_copies = exchange(5, lambda peer: back_send.at[peer], back_recv.at[me_ctx])
    back_recv[me_ctx] = back_send[me_ctx]
    multiply(gated_spec, grad_spec, True)
    invert(lag_send)
    lag_copies = exchange(6, lambda peer: lag_send.at[peer], lag_recv.at[me_ctx])
    lag_recv[me_ctx] = lag_send[me_ctx]
    for distance in range(2, lines - 1):
        chain_take(distance)
    arrived(back_copies)

    def conv_gradient(tile, carry):
        cols = column(tile)
        back = per_part_view(back_recv, tile)
        grad_conv[0, 0:block_len, cols] = grad_mixed[:, cols] * per_part_view(long_recv, tile)
        grad_conv[1, 0:block_len, cols] = back * conv[2, :, cols]
        grad_conv[2, 0:block_len, cols] = back * conv[1, :, cols]
        return carry

    lax.fori_loop(0, chans // TILE, conv_gradient, 0)
    next_copy = remote(
        grad_conv.at[:, pl.ds(0, NEXT_EDGE), :],
        next_edge_in,
        next_sems,
        0,
        lax.rem(me_ctx + n_ctx - 1, n_ctx),
        me_ch,
    )
    next_copy.start()

    def tap_gradient(tile, carry):
        cols = column(tile)
        for branch in range(3):
            values = grad_conv[branch, 0:block_len, cols]
            for tap in range(taps):
                term = values * extended[branch, EDGE - tap : EDGE - tap + block_len, cols]
                kernel_parts[me_ctx, branch, tap : tap + 1, cols] = jnp.sum(
                    term, axis=0, keepdims=True
                )
            kernel_parts[me_ctx, branch, taps : taps + 1, cols] = jnp.zeros((1, TILE), F32)
        return carry

    lax.fori_loop(0, chans // TILE, tap_gradient, 0)
    kernel_copies = exchange(7, lambda peer: kernel_parts.at[me_ctx], kernel_parts.at[me_ctx])
    chain_take(lines - 1)
    next_copy.wait()

    def feature_gradient(tile, carry):
        cols = column(tile)
        for branch in range(3):
            grad_conv[branch, block_len : block_len + NEXT_EDGE, cols] = jnp.where(
                me_ctx < n_ctx - 1, next_edge_in[branch, :, cols], 0.0
            )
            total = None
            for tap in range(taps):
                term = (
                    short_kernel[branch, tap : tap + 1, cols]
                    * grad_conv[branch, tap : tap + block_len, cols]
                )
                total = term if total is None else total + term
            grad_features[branch, :, cols] = total.astype(BF16)
        return carry

    lax.fori_loop(0, chans // TILE, feature_gradient, 0)

    forward_copies = []
    for source in range(n_ctx):
        @pl.when(me_ctx == source)
        def _():
            own_relay.wait()

        @pl.when(me_ctx != source)
        def _(source=source):
            slot = all_mixed.at[core, source]
            remote(line_mixed.at[0], slot, relay_sems, source, me_ctx, me_ch).wait_recv()

        copy = remote(
            all_mixed.at[core, source],
            all_mixed.at[core, source],
            forward_sems,
            source,
            me_ctx,
            z * 2 + 1 - core,
        )
        copy.start()
        forward_copies.append(copy)

    arrived(lag_copies)

    def filter_gradient(tile, carry):
        grad_filter[:, column(tile)] = per_part_view(lag_recv, tile)
        return carry

    lax.fori_loop(0, chans // TILE, filter_gradient, 0)
    arrived(kernel_copies)
    total = kernel_parts[0]
    for index in range(1, n_ctx):
        total = total + kernel_parts[index]
    grad_kernel[...] = total[:, :taps, :]
    arrived(grad_out_copies)
    own_grad_out.wait()
    for copy in forward_copies:
        copy.wait()
    edge_copy.wait_send()
    for copies in (
        filter_copies,
        gated_copies,
        long_copies,
        grad_out_copies,
        grad_copies,
        back_copies,
        lag_copies,
        kernel_copies,
        pair_copies,
        line_copies,
    ):
        for copy in copies:
            copy.wait_send()
    for distance in range(1, lines):
        for sign in (1, -1):

            @pl.when(chain_sends(sign, distance))
            def _(sign=sign, distance=distance):
                chain_copy(sign, distance).wait_send()

    for block in range(lines):

        @pl.when(me_ctx != block)
        def _(block=block):
            relay_copy(block).wait_send()


def product_kernel(
    mixed_tile,
    all_grad_out,
    features_from,
    kernel_from,
    filter_from,
    grad_weight,
    features_to,
    kernel_to,
    filter_to,
    sems,
):
    step, steps = pl.program_id(0), pl.num_programs(0)
    pairs = [(features_from, features_to), (kernel_from, kernel_to), (filter_from, filter_to)]
    copies = [
        pltpu.make_async_copy(source, target, sems.at[index])
        for index, (source, target) in enumerate(pairs)
    ]

    @pl.when(step == 0)
    def _():
        for copy in copies:
            copy.start()

    grad_weight[...] = lax.dot_general(
        mixed_tile[0],
        all_grad_out[...],
        (((0,), (0,)), ((), ())),
        preferred_element_type=F32,
    )

    @pl.when(step == steps - 1)
    def _():
        for copy in copies:
            copy.wait()


def fused(features, short_kernel, long_filter, out_weight, grad_out):
    block_len, chans = grad_out.shape
    taps = short_kernel.shape[1]
    n_ctx, lines = lax.axis_size("ctx"), lax.axis_size("ch") // 2
    part, length = chans // n_ctx, n_ctx * block_len
    tables = [jnp.asarray(table) for table in fourier_tables(length)]
    in_vmem = pl.BlockSpec(memory_space=pltpu.VMEM)
    in_place = pl.BlockSpec(memory_space=pl.ANY)
    staged = pltpu.VMEM((n_ctx, block_len, part), BF16)
    wide = pltpu.VMEM((length, part), BF16)
    spectra = pltpu.VMEM((2 * length, part), F32)
    blocks = pltpu.VMEM((lines, block_len, chans), BF16)
    scratch = [
        pltpu.VMEM((W_SLOTS, chans, chans), BF16),
        blocks,
        blocks,
        pltpu.VMEM((lines, block_len, chans), F32),
        blocks,
        blocks,
        pltpu.VMEM((3, EDGE, chans), BF16),
        pltpu.VMEM((3, EDGE + block_len, chans), F32),
        pltpu.VMEM((3, block_len, chans), F32),
        staged,
        staged,
        staged,
        wide,
        wide,
        wide,
        spectra,
        spectra,
        spectra,
        pltpu.VMEM((2 * length, part), BF16),
        pltpu.VMEM((2 * length, part), BF16),
        staged,
        staged,
        staged,
        staged,
        staged,
        staged,
        blocks,
        pltpu.VMEM((block_len, chans), F32),
        pltpu.VMEM((3, block_len + NEXT_EDGE, chans), F32),
        pltpu.VMEM((3, NEXT_EDGE, chans), F32),
        pltpu.VMEM((n_ctx, 3, taps + 1, chans), F32),
        pltpu.SemaphoreType.DMA((W_SLOTS,)),
        pltpu.SemaphoreType.DMA((2,)),
        pltpu.SemaphoreType.DMA((2, lines)),
        pltpu.SemaphoreType.DMA((2, lines)),
        pltpu.SemaphoreType.DMA((2, 1)),
        pltpu.SemaphoreType.DMA((2, 1)),
        pltpu.SemaphoreType.DMA((8, 2, n_ctx - 1)),
        pltpu.SemaphoreType.DMA((2, 2, lines - 1)),
        pltpu.SemaphoreType.DMA((2, lines)),
        pltpu.SemaphoreType.DMA((2, n_ctx)),
    ]
    grad_features, grad_kernel, grad_filter, all_grad_out, all_mixed = pl.pallas_call(
        fused_kernel,
        out_shape=[
            jax.ShapeDtypeStruct(features.shape, BF16),
            jax.ShapeDtypeStruct(short_kernel.shape, F32),
            jax.ShapeDtypeStruct(long_filter.shape, F32),
            jax.ShapeDtypeStruct((n_ctx, block_len, chans), BF16),
            jax.ShapeDtypeStruct((2, n_ctx, block_len, chans), BF16),
        ],
        in_specs=[in_vmem, in_vmem, in_vmem, in_place] + [in_vmem] * 5,
        out_specs=[in_vmem, in_vmem, in_vmem, in_place, in_place],
        scratch_shapes=scratch,
        compiler_params=pltpu.CompilerParams(
            collective_id=0, has_side_effects=True, vmem_limit_bytes=56 * 1024 * 1024
        ),
        cost_estimate=pl.CostEstimate(
            flops=8 * 10**9, bytes_accessed=28 * 2**20, transcendentals=0
        ),
    )(features, short_kernel, long_filter, out_weight, grad_out, *tables)
    per_half = chans // ROWS
    grad_weight, grad_features, grad_kernel, grad_filter = pl.pallas_call(
        product_kernel,
        grid=(2 * per_half,),
        out_shape=[
            jax.ShapeDtypeStruct((2 * chans, chans), F32),
            jax.ShapeDtypeStruct(grad_features.shape, BF16),
            jax.ShapeDtypeStruct(grad_kernel.shape, F32),
            jax.ShapeDtypeStruct(grad_filter.shape, F32),
        ],
        in_specs=[
            pl.BlockSpec((1, length, ROWS), lambda i: (i // per_half, 0, lax.rem(i, per_half))),
            pl.BlockSpec((length, chans), lambda i: (0, 0)),
            in_place,
            in_place,
            in_place,
        ],
        out_specs=[
            pl.BlockSpec((ROWS, chans), lambda i: (i, 0)),
            in_place,
            in_place,
            in_place,
        ],
        scratch_shapes=[pltpu.SemaphoreType.DMA((3,))],
        compiler_params=pltpu.CompilerParams(vmem_limit_bytes=32 * 1024 * 1024),
        cost_estimate=pl.CostEstimate(
            flops=4 * 10**9, bytes_accessed=12 * 2**20, transcendentals=0
        ),
    )(
        all_mixed.reshape(2, length, chans),
        all_grad_out.reshape(length, chans),
        grad_features,
        grad_kernel,
        grad_filter,
    )
    return (grad_features, grad_kernel, grad_filter, grad_weight)


def solution(mesh):
    n_ctx, n_ch = mesh.shape["ctx"], mesh.shape["ch"]

    def local(features, short_kernel, long_filter, out_weight, grad_out):
        aligned = grad_out.shape[1] % (TILE * n_ctx) == 0 and grad_out.shape[1] % ROWS == 0
        body = fused if n_ch == 2 * n_ctx and aligned else plain
        return body(features, short_kernel, long_filter, out_weight, grad_out)

    return jax.shard_map(
        local,
        mesh=mesh,
        in_specs=(
            P(None, "ctx", "ch"),
            P(None, None, "ch"),
            P("ctx", "ch"),
            P(None, "ch"),
            P("ctx", "ch"),
        ),
        out_specs=(P(None, "ctx", "ch"), P(None, None, "ch"), P("ctx", "ch"), P("ctx", "ch")),
        check_vma=False,
    )
```

```python
import numpy as np

import jax
import jax.numpy as jnp
from jax import lax
from jax.experimental import pallas as pl
from jax.experimental.pallas import tpu as pltpu
from jax.sharding import PartitionSpec as P

BF16 = jnp.bfloat16
F32 = jnp.float32


def fourier_tables(length):
    period = 2 * length
    freq = np.arange(length)
    angles = (freq[:, None] * np.arange(length)[None, :] % period) * (2 * np.pi / period)
    cos_part, sin_part = np.cos(angles), -np.sin(angles)
    sin_part[0] = 1 - 2 * (np.arange(length) % 2)
    ahead = np.concatenate([cos_part, sin_part], axis=0)
    weight = np.full((length, 1), 2.0 / period)
    weight[0] = 1.0 / period
    back = np.concatenate([cos_part * weight, sin_part * weight], axis=0).T

    def halves(table):
        high = table.astype(np.float32).astype(BF16)
        low = (table - high.astype(np.float64)).astype(np.float32).astype(BF16)
        return high, low

    return halves(ahead) + halves(back)


def to_spectrum(high, low, block):
    return jnp.dot(high, block, preferred_element_type=F32) + jnp.dot(
        low, block, preferred_element_type=F32
    )


def from_spectrum(high, low, real_part, imag_part):
    half = real_part.shape[0]
    total = None
    for values, columns in ((real_part, slice(0, half)), (imag_part, slice(half, 2 * half))):
        upper = values.astype(BF16)
        rest = (values - upper.astype(F32)).astype(BF16)
        term = (
            jnp.dot(high[:, columns], upper, preferred_element_type=F32)
            + jnp.dot(low[:, columns], upper, preferred_element_type=F32)
            + jnp.dot(high[:, columns], rest, preferred_element_type=F32)
        )
        total = term if total is None else total + term
    return total


def spectral_product(first, second, conjugate):
    half = first.shape[0] // 2
    first_real, first_imag = first[:half], first[half:]
    second_real, second_imag = second[:half], second[half:]
    edge = lax.broadcasted_iota(jnp.int32, first_real.shape, 0) == 0
    real_real = first_real * second_real
    imag_imag = first_imag * second_imag
    if conjugate:
        real_part = real_real + imag_imag
        imag_part = first_real * second_imag - first_imag * second_real
    else:
        real_part = real_real - imag_imag
        imag_part = first_real * second_imag + first_imag * second_real
    return jnp.where(edge, real_real, real_part), jnp.where(edge, imag_imag, imag_part)


def shifted(array, axis, by):
    peers = lax.axis_size(axis)
    pairs = [(i, i + by) for i in range(peers) if 0 <= i + by < peers]
    return lax.ppermute(array, axis, pairs)


def whole_sequence(block):
    return lax.all_to_all(block, "ctx", split_axis=1, concat_axis=0, tiled=True)


def own_tokens(block):
    return lax.all_to_all(block, "ctx", split_axis=0, concat_axis=1, tiled=True)


def plain(features, short_kernel, long_filter, out_weight, grad_out):
    block_len, chans = features.shape[1:]
    taps = short_kernel.shape[1]
    margin = taps - 1
    ahead_high, ahead_low, back_high, back_low = fourier_tables(block_len * lax.axis_size("ctx"))
    partial_mixed = jnp.einsum("tc,dc->td", grad_out, out_weight, preferred_element_type=F32)
    grad_mixed = lax.psum_scatter(partial_mixed, "ch", scatter_dimension=1, tiled=True)
    before = shifted(features[:, block_len - margin :, :], "ctx", 1)
    extended = jnp.concatenate([before, features], axis=1).astype(F32)
    conv = jnp.zeros((3, block_len, chans), F32)
    for tap_index in range(taps):
        conv = (
            conv
            + short_kernel[:, tap_index, None, :]
            * extended[:, margin - tap_index : margin - tap_index + block_len, :]
        )
    q_conv, k_conv, v_conv = (conv[0], conv[1], conv[2])
    gated = (k_conv * v_conv).astype(BF16)
    filter_spec = to_spectrum(ahead_high, ahead_low, whole_sequence(long_filter))
    gated_spec = to_spectrum(ahead_high, ahead_low, whole_sequence(gated))
    out_spec = spectral_product(filter_spec, gated_spec, False)
    long_out = own_tokens(from_spectrum(back_high, back_low, *out_spec))
    mixed = (q_conv * long_out).astype(BF16)
    grad_long = (grad_mixed * q_conv).astype(BF16)
    grad_spec = to_spectrum(ahead_high, ahead_low, whole_sequence(grad_long))
    back_spec = spectral_product(filter_spec, grad_spec, True)
    grad_gated = own_tokens(from_spectrum(back_high, back_low, *back_spec))
    lag_spec = spectral_product(gated_spec, grad_spec, True)
    grad_filter = own_tokens(from_spectrum(back_high, back_low, *lag_spec))
    grad_conv = jnp.stack([grad_mixed * long_out, grad_gated * v_conv, grad_gated * k_conv], axis=0)
    after = shifted(grad_conv[:, :margin, :], "ctx", -1)
    grad_extended = jnp.concatenate([grad_conv, after], axis=1)
    feature_total = jnp.zeros((3, block_len, chans), F32)
    kernel_rows = []
    for tap_index in range(taps):
        feature_total = (
            feature_total
            + short_kernel[:, tap_index, None, :]
            * grad_extended[:, tap_index : tap_index + block_len, :]
        )
        kernel_rows.append(
            jnp.sum(
                grad_conv * extended[:, margin - tap_index : margin - tap_index + block_len, :],
                axis=1,
            )
        )
    grad_features = feature_total.astype(BF16)
    grad_kernel = lax.psum(jnp.stack(kernel_rows, axis=1), "ctx")
    all_mixed = whole_sequence(lax.all_gather(mixed, "ch", axis=1, tiled=True))
    all_grad_out = lax.all_gather(grad_out, "ctx", axis=0, tiled=True)
    grad_weight = jnp.einsum("tn,tc->nc", all_mixed, all_grad_out, preferred_element_type=F32)
    return (grad_features, grad_kernel, grad_filter, grad_weight)


MESH = pl.DeviceIdType.MESH
EDGE = 16
NEXT_EDGE = 8
TILE = 128
ROWS = 256
W_SLOTS = 3


def fused_kernel(
    features,
    short_kernel,
    long_filter,
    out_weight,
    grad_out,
    ahead_high,
    ahead_low,
    back_high,
    back_low,
    grad_features,
    grad_kernel,
    grad_filter,
    all_grad_out,
    all_mixed,
    w_buf,
    pair_out,
    pair_in,
    partials,
    line_out,
    line_in,
    edge_in,
    extended,
    conv,
    filter_out,
    gated_out,
    grad_long_out,
    filter_wide,
    gated_wide,
    grad_wide,
    filter_spec,
    gated_spec,
    grad_spec,
    prod_high,
    prod_low,
    long_send,
    long_recv,
    back_send,
    back_recv,
    lag_send,
    lag_recv,
    line_mixed,
    grad_conv,
    next_edge_in,
    kernel_parts,
    w_sem,
    local_sem,
    pair_sems,
    line_sems,
    edge_sems,
    next_sems,
    exchange_sems,
    chain_sems,
    relay_sems,
    forward_sems,
):
    me_ctx, me_ch = lax.axis_index("ctx"), lax.axis_index("ch")
    n_ctx, lines = lax.axis_size("ctx"), lax.axis_size("ch") // 2
    core, z = lax.rem(me_ch, 2), me_ch // 2
    block_len, chans = grad_out.shape
    taps = short_kernel.shape[1]
    part = chans // n_ctx
    length = n_ctx * block_len
    hops = [k % lines for k in range(1, lines + 1)]

    def column(index):
        return pl.ds(pl.multiple_of(index * TILE, TILE), TILE)

    def token_rows(index):
        return pl.ds(pl.multiple_of(index * block_len, block_len), block_len)

    def remote(src, dst, sems, index, ctx, ch):
        return pltpu.make_async_remote_copy(
            src_ref=src,
            dst_ref=dst,
            send_sem=sems.at[0, index],
            recv_sem=sems.at[1, index],
            device_id={"ctx": ctx, "ch": ch},
            device_id_type=MESH,
        )

    weight_steps = []
    for k in hops:
        target = lax.rem(z + k, lines) * 2
        weight_steps += [target + 1 - core, target + core]

    def weight_copy(step):
        slot = step % W_SLOTS
        start = pl.multiple_of(weight_steps[step] * chans, chans)
        return pltpu.make_async_copy(
            out_weight.at[pl.ds(start, chans), :], w_buf.at[slot], w_sem.at[slot]
        )

    for step in range(W_SLOTS):
        weight_copy(step).start()

    barrier = pltpu.get_barrier_semaphore()
    greeted = [(lax.rem(me_ctx + d, n_ctx), me_ch) for d in range(1, n_ctx)]
    greeted += [(me_ctx, lax.rem(z + d, lines) * 2 + core) for d in range(1, lines)]
    greeted.append((me_ctx, z * 2 + 1 - core))
    for ctx, ch in greeted:
        pl.semaphore_signal(
            barrier, inc=1, device_id={"ctx": ctx, "ch": ch}, device_id_type=MESH
        )

    def stage_filter(tile, carry):
        per_part = part // TILE
        filter_out[tile // per_part, :, column(lax.rem(tile, per_part))] = long_filter[
            :, column(tile)
        ]
        return carry

    lax.fori_loop(0, chans // TILE, stage_filter, 0)
    filter_wide[token_rows(me_ctx), :] = filter_out[me_ctx]
    pl.semaphore_wait(barrier, len(greeted))

    def exchange(number, src_at, dst):
        copies = []
        for distance in range(1, n_ctx):
            peer = lax.rem(me_ctx + distance, n_ctx)
            copies.append(
                remote(
                    src_at(peer),
                    dst,
                    exchange_sems.at[number],
                    distance - 1,
                    peer,
                    me_ch,
                )
            )
        for copy in copies:
            copy.start()
        return copies

    def arrived(copies):
        for copy in copies:
            copy.wait_recv()

    edge_copy = remote(
        features.at[:, pl.ds(block_len - EDGE, EDGE), :],
        edge_in,
        edge_sems,
        0,
        lax.rem(me_ctx + 1, n_ctx),
        me_ch,
    )
    edge_copy.start()
    filter_copies = exchange(0, lambda peer: filter_out.at[peer], filter_wide.at[token_rows(me_ctx)])

    pair_copies, line_copies = [], []

    def finish_hop(index):
        pair_copies[index].wait_recv()
        if hops[index] == 0:
            partials[index] = partials[index] + pair_in[index].astype(F32)
            return
        line_out[index] = (partials[index] + pair_in[index].astype(F32)).astype(BF16)
        copy = remote(
            line_out.at[index],
            line_in.at[index],
            line_sems,
            index,
            me_ctx,
            lax.rem(z + hops[index], lines) * 2 + core,
        )
        copy.start()
        line_copies.append(copy)

    for step in range(2 * lines):
        index = step // 2
        slot = step % W_SLOTS
        weight_copy(step).wait()

        def project(tile, carry, step=step, index=index, slot=slot):
            rows = pl.ds(pl.multiple_of(tile * ROWS, ROWS), ROWS)
            value = lax.dot_general(
                grad_out[...],
                w_buf[slot, rows, :],
                (((1,), (1,)), ((), ())),
                preferred_element_type=F32,
            )
            if step % 2 == 0:
                pair_out[index, :, rows] = value.astype(BF16)
            else:
                partials[index, :, rows] = value
            return carry

        lax.fori_loop(0, chans // ROWS, project, 0)
        if step + W_SLOTS < 2 * lines:
            weight_copy(step + W_SLOTS).start()
        if step % 2 == 0:
            copy = remote(
                pair_out.at[index], pair_in.at[index], pair_sems, index, me_ctx, z * 2 + 1 - core
            )
            copy.start()
            pair_copies.append(copy)
            if index >= 1:
                finish_hop(index - 1)

    edge_copy.wait_recv()

    def convolve(tile, carry):
        cols = column(tile)
        totals = []
        for branch in range(3):
            edge = edge_in[branch, :, cols].astype(F32)
            extended[branch, 0:EDGE, cols] = jnp.where(me_ctx > 0, edge, 0.0)
            extended[branch, EDGE : EDGE + block_len, cols] = features[branch, :, cols].astype(F32)
            total = None
            for tap in range(taps):
                term = (
                    short_kernel[branch, tap : tap + 1, cols]
                    * extended[branch, EDGE - tap : EDGE - tap + block_len, cols]
                )
                total = term if total is None else total + term
            conv[branch, :, cols] = total
            totals.append(total)
        per_part = part // TILE
        gated_out[tile // per_part, :, column(lax.rem(tile, per_part))] = (
            totals[1] * totals[2]
        ).astype(BF16)
        return carry

    lax.fori_loop(0, chans // TILE, convolve, 0)
    gated_copies = exchange(1, lambda peer: gated_out.at[peer], gated_wide.at[token_rows(me_ctx)])
    gated_wide[token_rows(me_ctx), :] = gated_out[me_ctx]
    finish_hop(lines - 1)
    own_grad_out = pltpu.make_async_copy(grad_out, all_grad_out.at[me_ctx], local_sem.at[0])
    own_grad_out.start()

    def transform(source, target):
        def body(tile, carry):
            rows = pl.ds(pl.multiple_of(tile * ROWS, ROWS), ROWS)
            target[rows, :] = to_spectrum(ahead_high[rows, :], ahead_low[rows, :], source[...])
            return carry

        lax.fori_loop(0, 2 * length // ROWS, body, 0)

    def multiply(first, second, conjugate):
        step_rows = 32

        def body(tile, carry):
            upper = pl.ds(pl.multiple_of(tile * step_rows, step_rows), step_rows)
            lower = pl.ds(pl.multiple_of(length + tile * step_rows, step_rows), step_rows)
            first_real, first_imag = first[upper, :], first[lower, :]
            second_real, second_imag = second[upper, :], second[lower, :]
            row = lax.broadcasted_iota(jnp.int32, first_real.shape, 0) + tile * step_rows
            edge = row == 0
            real_real = first_real * second_real
            imag_imag = first_imag * second_imag
            if conjugate:
                real_part = real_real + imag_imag
                imag_part = first_real * second_imag - first_imag * second_real
            else:
                real_part = real_real - imag_imag
                imag_part = first_real * second_imag + first_imag * second_real
            for rows, value in (
                (upper, jnp.where(edge, real_real, real_part)),
                (lower, jnp.where(edge, imag_imag, imag_part)),
            ):
                high = value.astype(BF16)
                prod_high[rows, :] = high
                prod_low[rows, :] = (value - high.astype(F32)).astype(BF16)
            return carry

        lax.fori_loop(0, length // step_rows, body, 0)

    def invert(target):
        def body(tile, carry):
            rows = token_rows(tile)
            high, low = back_high[rows, :], back_low[rows, :]
            target[tile] = (
                jnp.dot(high, prod_high[...], preferred_element_type=F32)
                + jnp.dot(low, prod_high[...], preferred_element_type=F32)
                + jnp.dot(high, prod_low[...], preferred_element_type=F32)
            ).astype(BF16)
            return carry

        lax.fori_loop(0, n_ctx, body, 0)

    arrived(filter_copies)
    transform(filter_wide, filter_spec)
    arrived(gated_copies)
    transform(gated_wide, gated_spec)
    multiply(filter_spec, gated_spec, False)
    invert(long_send)
    long_copies = exchange(2, lambda peer: long_send.at[peer], long_recv.at[me_ctx])
    long_recv[me_ctx] = long_send[me_ctx]
    grad_out_copies = exchange(3, lambda peer: grad_out, all_grad_out.at[me_ctx])

    arrived(long_copies)

    def per_part_view(ref, tile):
        per_part = part // TILE
        return ref[tile // per_part, :, column(lax.rem(tile, per_part))].astype(F32)

    def mix(tile, carry):
        cols = column(tile)
        line_mixed[z, :, cols] = (conv[0, :, cols] * per_part_view(long_recv, tile)).astype(BF16)
        return carry

    lax.fori_loop(0, chans // TILE, mix, 0)

    def chain_copy(sign, distance):
        block = line_mixed.at[z - sign * (distance - 1)]
        way = 0 if sign > 0 else 1
        return remote(
            block, block, chain_sems.at[way], distance - 1, me_ctx, (z + sign) * 2 + core
        )

    def chain_sends(sign, distance):
        first, after = z - sign * (distance - 1), z + sign
        inside = jnp.logical_and(first >= 0, first < lines)
        return jnp.logical_and(inside, jnp.logical_and(after >= 0, after < lines))

    def chain_receives(sign, distance):
        first = z - sign * distance
        return jnp.logical_and(first >= 0, first < lines)

    own_relay = pltpu.make_async_copy(
        line_mixed.at[me_ctx], all_mixed.at[core, me_ctx], local_sem.at[1]
    )

    def relay_copy(block):
        return pltpu.make_async_remote_copy(
            src_ref=line_mixed.at[block],
            dst_ref=all_mixed.at[core, me_ctx],
            send_sem=relay_sems.at[0, block],
            recv_sem=relay_sems.at[1, me_ctx],
            device_id={"ctx": block, "ch": me_ch},
            device_id_type=MESH,
        )

    def relay(block):
        @pl.when(block == me_ctx)
        def _():
            own_relay.start()

        @pl.when(block != me_ctx)
        def _():
            relay_copy(block).start()

    def chain_start(distance):
        for sign in (1, -1):

            @pl.when(chain_sends(sign, distance))
            def _(sign=sign):
                chain_copy(sign, distance).start()

    def chain_take(distance):
        for sign in (1, -1):

            @pl.when(chain_receives(sign, distance))
            def _(sign=sign):
                chain_copy(sign, distance).wait_recv()

        if distance + 1 < lines:
            chain_start(distance + 1)
        for sign in (1, -1):

            @pl.when(chain_receives(sign, distance))
            def _(sign=sign):
                relay(z - sign * distance)

    chain_start(1)
    relay(z)
    for copy in line_copies:
        copy.wait_recv()

    def take_grad(tile, carry):
        cols = column(tile)
        total = partials[lines - 1, :, cols]
        for index in range(lines - 1):
            total = total + line_in[index, :, cols].astype(F32)
        grad_conv[0, 0:block_len, cols] = total * per_part_view(long_recv, tile)
        per_part = part // TILE
        grad_long_out[tile // per_part, :, column(lax.rem(tile, per_part))] = (
            total * conv[0, :, cols]
        ).astype(BF16)
        return carry

    lax.fori_loop(0, chans // TILE, take_grad, 0)
    grad_copies = exchange(
        4, lambda peer: grad_long_out.at[peer], grad_wide.at[token_rows(me_ctx)]
    )
    grad_wide[token_rows(me_ctx), :] = grad_long_out[me_ctx]

    def tap_gradient(branches):
        def body(tile, carry):
            cols = column(tile)
            for branch in branches:
                values = grad_conv[branch, 0:block_len, cols]
                for tap in range(taps):
                    term = values * extended[branch, EDGE - tap : EDGE - tap + block_len, cols]
                    kernel_parts[me_ctx, branch, tap : tap + 1, cols] = jnp.sum(
                        term, axis=0, keepdims=True
                    )
                kernel_parts[me_ctx, branch, taps : taps + 1, cols] = jnp.zeros((1, TILE), F32)
            return carry

        return body

    lax.fori_loop(0, chans // TILE, tap_gradient((0,)), 0)
    chain_take(1)
    arrived(grad_copies)
    transform(grad_wide, grad_spec)
    multiply(filter_spec, grad_spec, True)
    invert(back_send)
    back_copies = exchange(5, lambda peer: back_send.at[peer], back_recv.at[me_ctx])
    back_recv[me_ctx] = back_send[me_ctx]
    multiply(gated_spec, grad_spec, True)
    invert(lag_send)
    lag_copies = exchange(6, lambda peer: lag_send.at[peer], lag_recv.at[me_ctx])
    lag_recv[me_ctx] = lag_send[me_ctx]
    for distance in range(2, lines - 1):
        chain_take(distance)
    arrived(back_copies)

    def conv_gradient(tile, carry):
        cols = column(tile)
        back = per_part_view(back_recv, tile)
        grad_conv[1, 0:block_len, cols] = back * conv[2, :, cols]
        grad_conv[2, 0:block_len, cols] = back * conv[1, :, cols]
        return carry

    lax.fori_loop(0, chans // TILE, conv_gradient, 0)
    next_copy = remote(
        grad_conv.at[:, pl.ds(0, NEXT_EDGE), :],
        next_edge_in,
        next_sems,
        0,
        lax.rem(me_ctx + n_ctx - 1, n_ctx),
        me_ch,
    )
    next_copy.start()

    chain_take(lines - 1)
    lax.fori_loop(0, chans // TILE, tap_gradient((1, 2)), 0)
    kernel_copies = exchange(7, lambda peer: kernel_parts.at[me_ctx], kernel_parts.at[me_ctx])
    next_copy.wait()

    forward_copies = []
    for source in range(n_ctx):
        @pl.when(me_ctx == source)
        def _():
            own_relay.wait()

        @pl.when(me_ctx != source)
        def _(source=source):
            slot = all_mixed.at[core, source]
            remote(line_mixed.at[0], slot, relay_sems, source, me_ctx, me_ch).wait_recv()

        copy = remote(
            all_mixed.at[core, source],
            all_mixed.at[core, source],
            forward_sems,
            source,
            me_ctx,
            z * 2 + 1 - core,
        )
        copy.start()
        forward_copies.append(copy)

    def feature_gradient(tile, carry):
        cols = column(tile)
        for branch in range(3):
            grad_conv[branch, block_len : block_len + NEXT_EDGE, cols] = jnp.where(
                me_ctx < n_ctx - 1, next_edge_in[branch, :, cols], 0.0
            )
            total = None
            for tap in range(taps):
                term = (
                    short_kernel[branch, tap : tap + 1, cols]
                    * grad_conv[branch, tap : tap + block_len, cols]
                )
                total = term if total is None else total + term
            grad_features[branch, :, cols] = total.astype(BF16)
        return carry

    lax.fori_loop(0, chans // TILE, feature_gradient, 0)

    arrived(lag_copies)

    def filter_gradient(tile, carry):
        grad_filter[:, column(tile)] = per_part_view(lag_recv, tile)
        return carry

    lax.fori_loop(0, chans // TILE, filter_gradient, 0)
    arrived(kernel_copies)
    total = kernel_parts[0]
    for index in range(1, n_ctx):
        total = total + kernel_parts[index]
    grad_kernel[...] = total[:, :taps, :]
    arrived(grad_out_copies)
    own_grad_out.wait()
    for copy in forward_copies:
        copy.wait()
    edge_copy.wait_send()
    for copies in (
        filter_copies,
        gated_copies,
        long_copies,
        grad_out_copies,
        grad_copies,
        back_copies,
        lag_copies,
        kernel_copies,
        pair_copies,
        line_copies,
    ):
        for copy in copies:
            copy.wait_send()
    for distance in range(1, lines):
        for sign in (1, -1):

            @pl.when(chain_sends(sign, distance))
            def _(sign=sign, distance=distance):
                chain_copy(sign, distance).wait_send()

    for block in range(lines):

        @pl.when(me_ctx != block)
        def _(block=block):
            relay_copy(block).wait_send()


def product_kernel(
    mixed_tile,
    all_grad_out,
    features_from,
    kernel_from,
    filter_from,
    grad_weight,
    features_to,
    kernel_to,
    filter_to,
    sems,
):
    step, steps = pl.program_id(0), pl.num_programs(0)
    pairs = [(features_from, features_to), (kernel_from, kernel_to), (filter_from, filter_to)]
    copies = [
        pltpu.make_async_copy(source, target, sems.at[index])
        for index, (source, target) in enumerate(pairs)
    ]

    @pl.when(step == 0)
    def _():
        for copy in copies:
            copy.start()

    grad_weight[...] = lax.dot_general(
        mixed_tile[0],
        all_grad_out[...],
        (((0,), (0,)), ((), ())),
        preferred_element_type=F32,
    )

    @pl.when(step == steps - 1)
    def _():
        for copy in copies:
            copy.wait()


def fused(features, short_kernel, long_filter, out_weight, grad_out):
    block_len, chans = grad_out.shape
    taps = short_kernel.shape[1]
    n_ctx, lines = lax.axis_size("ctx"), lax.axis_size("ch") // 2
    part, length = chans // n_ctx, n_ctx * block_len
    tables = [jnp.asarray(table) for table in fourier_tables(length)]
    in_vmem = pl.BlockSpec(memory_space=pltpu.VMEM)
    in_place = pl.BlockSpec(memory_space=pl.ANY)
    staged = pltpu.VMEM((n_ctx, block_len, part), BF16)
    wide = pltpu.VMEM((length, part), BF16)
    spectra = pltpu.VMEM((2 * length, part), F32)
    blocks = pltpu.VMEM((lines, block_len, chans), BF16)
    scratch = [
        pltpu.VMEM((W_SLOTS, chans, chans), BF16),
        blocks,
        blocks,
        pltpu.VMEM((lines, block_len, chans), F32),
        blocks,
        blocks,
        pltpu.VMEM((3, EDGE, chans), BF16),
        pltpu.VMEM((3, EDGE + block_len, chans), F32),
        pltpu.VMEM((3, block_len, chans), F32),
        staged,
        staged,
        staged,
        wide,
        wide,
        wide,
        spectra,
        spectra,
        spectra,
        pltpu.VMEM((2 * length, part), BF16),
        pltpu.VMEM((2 * length, part), BF16),
        staged,
        staged,
        staged,
        staged,
        staged,
        staged,
        blocks,
        pltpu.VMEM((3, block_len + NEXT_EDGE, chans), F32),
        pltpu.VMEM((3, NEXT_EDGE, chans), F32),
        pltpu.VMEM((n_ctx, 3, taps + 1, chans), F32),
        pltpu.SemaphoreType.DMA((W_SLOTS,)),
        pltpu.SemaphoreType.DMA((2,)),
        pltpu.SemaphoreType.DMA((2, lines)),
        pltpu.SemaphoreType.DMA((2, lines)),
        pltpu.SemaphoreType.DMA((2, 1)),
        pltpu.SemaphoreType.DMA((2, 1)),
        pltpu.SemaphoreType.DMA((8, 2, n_ctx - 1)),
        pltpu.SemaphoreType.DMA((2, 2, lines - 1)),
        pltpu.SemaphoreType.DMA((2, lines)),
        pltpu.SemaphoreType.DMA((2, n_ctx)),
    ]
    grad_features, grad_kernel, grad_filter, all_grad_out, all_mixed = pl.pallas_call(
        fused_kernel,
        out_shape=[
            jax.ShapeDtypeStruct(features.shape, BF16),
            jax.ShapeDtypeStruct(short_kernel.shape, F32),
            jax.ShapeDtypeStruct(long_filter.shape, F32),
            jax.ShapeDtypeStruct((n_ctx, block_len, chans), BF16),
            jax.ShapeDtypeStruct((2, n_ctx, block_len, chans), BF16),
        ],
        in_specs=[in_vmem, in_vmem, in_vmem, in_place] + [in_vmem] * 5,
        out_specs=[in_vmem, in_vmem, in_vmem, in_place, in_place],
        scratch_shapes=scratch,
        compiler_params=pltpu.CompilerParams(
            collective_id=0, has_side_effects=True, vmem_limit_bytes=56 * 1024 * 1024
        ),
        cost_estimate=pl.CostEstimate(
            flops=8 * 10**9, bytes_accessed=28 * 2**20, transcendentals=0
        ),
    )(features, short_kernel, long_filter, out_weight, grad_out, *tables)
    per_half = chans // ROWS
    grad_weight, grad_features, grad_kernel, grad_filter = pl.pallas_call(
        product_kernel,
        grid=(2 * per_half,),
        out_shape=[
            jax.ShapeDtypeStruct((2 * chans, chans), F32),
            jax.ShapeDtypeStruct(grad_features.shape, BF16),
            jax.ShapeDtypeStruct(grad_kernel.shape, F32),
            jax.ShapeDtypeStruct(grad_filter.shape, F32),
        ],
        in_specs=[
            pl.BlockSpec((1, length, ROWS), lambda i: (i // per_half, 0, lax.rem(i, per_half))),
            pl.BlockSpec((length, chans), lambda i: (0, 0)),
            in_place,
            in_place,
            in_place,
        ],
        out_specs=[
            pl.BlockSpec((ROWS, chans), lambda i: (i, 0)),
            in_place,
            in_place,
            in_place,
        ],
        scratch_shapes=[pltpu.SemaphoreType.DMA((3,))],
        compiler_params=pltpu.CompilerParams(vmem_limit_bytes=60 * 1024 * 1024),
        cost_estimate=pl.CostEstimate(
            flops=4 * 10**9, bytes_accessed=12 * 2**20, transcendentals=0
        ),
    )(
        all_mixed.reshape(2, length, chans),
        all_grad_out.reshape(length, chans),
        grad_features,
        grad_kernel,
        grad_filter,
    )
    return (grad_features, grad_kernel, grad_filter, grad_weight)


def solution(mesh):
    n_ctx, n_ch = mesh.shape["ctx"], mesh.shape["ch"]

    def local(features, short_kernel, long_filter, out_weight, grad_out):
        aligned = grad_out.shape[1] % (TILE * n_ctx) == 0 and grad_out.shape[1] % ROWS == 0
        body = fused if n_ch == 2 * n_ctx and aligned else plain
        return body(features, short_kernel, long_filter, out_weight, grad_out)

    return jax.shard_map(
        local,
        mesh=mesh,
        in_specs=(
            P(None, "ctx", "ch"),
            P(None, None, "ch"),
            P("ctx", "ch"),
            P(None, "ch"),
            P("ctx", "ch"),
        ),
        out_specs=(P(None, "ctx", "ch"), P(None, None, "ch"), P("ctx", "ch"), P("ctx", "ch")),
        check_vma=False,
    )
```

```python
import numpy as np

import jax
import jax.numpy as jnp
from jax import lax
from jax.experimental import pallas as pl
from jax.experimental.pallas import tpu as pltpu
from jax.sharding import PartitionSpec as P

BF16 = jnp.bfloat16
F32 = jnp.float32


def fourier_tables(length):
    period = 2 * length
    freq = np.arange(length)
    angles = (freq[:, None] * np.arange(length)[None, :] % period) * (2 * np.pi / period)
    cos_part, sin_part = np.cos(angles), -np.sin(angles)
    sin_part[0] = 1 - 2 * (np.arange(length) % 2)
    ahead = np.concatenate([cos_part, sin_part], axis=0)
    weight = np.full((length, 1), 2.0 / period)
    weight[0] = 1.0 / period
    back = np.concatenate([cos_part * weight, sin_part * weight], axis=0).T

    def halves(table):
        high = table.astype(np.float32).astype(BF16)
        low = (table - high.astype(np.float64)).astype(np.float32).astype(BF16)
        return high, low

    return halves(ahead) + halves(back)


def to_spectrum(high, low, block):
    return jnp.dot(high, block, preferred_element_type=F32) + jnp.dot(
        low, block, preferred_element_type=F32
    )


def from_spectrum(high, low, real_part, imag_part):
    half = real_part.shape[0]
    total = None
    for values, columns in ((real_part, slice(0, half)), (imag_part, slice(half, 2 * half))):
        upper = values.astype(BF16)
        rest = (values - upper.astype(F32)).astype(BF16)
        term = (
            jnp.dot(high[:, columns], upper, preferred_element_type=F32)
            + jnp.dot(low[:, columns], upper, preferred_element_type=F32)
            + jnp.dot(high[:, columns], rest, preferred_element_type=F32)
        )
        total = term if total is None else total + term
    return total


def spectral_product(first, second, conjugate):
    half = first.shape[0] // 2
    first_real, first_imag = first[:half], first[half:]
    second_real, second_imag = second[:half], second[half:]
    edge = lax.broadcasted_iota(jnp.int32, first_real.shape, 0) == 0
    real_real = first_real * second_real
    imag_imag = first_imag * second_imag
    if conjugate:
        real_part = real_real + imag_imag
        imag_part = first_real * second_imag - first_imag * second_real
    else:
        real_part = real_real - imag_imag
        imag_part = first_real * second_imag + first_imag * second_real
    return jnp.where(edge, real_real, real_part), jnp.where(edge, imag_imag, imag_part)


def shifted(array, axis, by):
    peers = lax.axis_size(axis)
    pairs = [(i, i + by) for i in range(peers) if 0 <= i + by < peers]
    return lax.ppermute(array, axis, pairs)


def whole_sequence(block):
    return lax.all_to_all(block, "ctx", split_axis=1, concat_axis=0, tiled=True)


def own_tokens(block):
    return lax.all_to_all(block, "ctx", split_axis=0, concat_axis=1, tiled=True)


def plain(features, short_kernel, long_filter, out_weight, grad_out):
    block_len, chans = features.shape[1:]
    taps = short_kernel.shape[1]
    margin = taps - 1
    ahead_high, ahead_low, back_high, back_low = fourier_tables(block_len * lax.axis_size("ctx"))
    partial_mixed = jnp.einsum("tc,dc->td", grad_out, out_weight, preferred_element_type=F32)
    grad_mixed = lax.psum_scatter(partial_mixed, "ch", scatter_dimension=1, tiled=True)
    before = shifted(features[:, block_len - margin :, :], "ctx", 1)
    extended = jnp.concatenate([before, features], axis=1).astype(F32)
    conv = jnp.zeros((3, block_len, chans), F32)
    for tap_index in range(taps):
        conv = (
            conv
            + short_kernel[:, tap_index, None, :]
            * extended[:, margin - tap_index : margin - tap_index + block_len, :]
        )
    q_conv, k_conv, v_conv = (conv[0], conv[1], conv[2])
    gated = (k_conv * v_conv).astype(BF16)
    filter_spec = to_spectrum(ahead_high, ahead_low, whole_sequence(long_filter))
    gated_spec = to_spectrum(ahead_high, ahead_low, whole_sequence(gated))
    out_spec = spectral_product(filter_spec, gated_spec, False)
    long_out = own_tokens(from_spectrum(back_high, back_low, *out_spec))
    mixed = (q_conv * long_out).astype(BF16)
    grad_long = (grad_mixed * q_conv).astype(BF16)
    grad_spec = to_spectrum(ahead_high, ahead_low, whole_sequence(grad_long))
    back_spec = spectral_product(filter_spec, grad_spec, True)
    grad_gated = own_tokens(from_spectrum(back_high, back_low, *back_spec))
    lag_spec = spectral_product(gated_spec, grad_spec, True)
    grad_filter = own_tokens(from_spectrum(back_high, back_low, *lag_spec))
    grad_conv = jnp.stack([grad_mixed * long_out, grad_gated * v_conv, grad_gated * k_conv], axis=0)
    after = shifted(grad_conv[:, :margin, :], "ctx", -1)
    grad_extended = jnp.concatenate([grad_conv, after], axis=1)
    feature_total = jnp.zeros((3, block_len, chans), F32)
    kernel_rows = []
    for tap_index in range(taps):
        feature_total = (
            feature_total
            + short_kernel[:, tap_index, None, :]
            * grad_extended[:, tap_index : tap_index + block_len, :]
        )
        kernel_rows.append(
            jnp.sum(
                grad_conv * extended[:, margin - tap_index : margin - tap_index + block_len, :],
                axis=1,
            )
        )
    grad_features = feature_total.astype(BF16)
    grad_kernel = lax.psum(jnp.stack(kernel_rows, axis=1), "ctx")
    all_mixed = whole_sequence(lax.all_gather(mixed, "ch", axis=1, tiled=True))
    all_grad_out = lax.all_gather(grad_out, "ctx", axis=0, tiled=True)
    grad_weight = jnp.einsum("tn,tc->nc", all_mixed, all_grad_out, preferred_element_type=F32)
    return (grad_features, grad_kernel, grad_filter, grad_weight)


MESH = pl.DeviceIdType.MESH
EDGE = 16
NEXT_EDGE = 8
TILE = 128
ROWS = 256
W_SLOTS = 3


def fused_kernel(
    features,
    short_kernel,
    long_filter,
    out_weight,
    grad_out,
    ahead_high,
    ahead_low,
    back_high,
    back_low,
    grad_features,
    grad_kernel,
    grad_filter,
    all_grad_out,
    all_mixed,
    w_buf,
    pair_out,
    pair_in,
    partials,
    line_out,
    line_in,
    edge_in,
    extended,
    conv,
    filter_out,
    gated_out,
    grad_long_out,
    filter_wide,
    gated_wide,
    grad_wide,
    filter_spec,
    gated_spec,
    grad_spec,
    prod_high,
    prod_low,
    long_send,
    long_recv,
    back_send,
    back_recv,
    lag_send,
    lag_recv,
    line_mixed,
    grad_conv,
    next_edge_in,
    kernel_parts,
    w_sem,
    local_sem,
    pair_sems,
    line_sems,
    edge_sems,
    next_sems,
    exchange_sems,
    chain_sems,
    relay_sems,
    forward_sems,
):
    me_ctx, me_ch = lax.axis_index("ctx"), lax.axis_index("ch")
    n_ctx, lines = lax.axis_size("ctx"), lax.axis_size("ch") // 2
    core, z = lax.rem(me_ch, 2), me_ch // 2
    block_len, chans = grad_out.shape
    taps = short_kernel.shape[1]
    part = chans // n_ctx
    length = n_ctx * block_len
    hops = [k % lines for k in range(1, lines + 1)]

    def column(index):
        return pl.ds(pl.multiple_of(index * TILE, TILE), TILE)

    def token_rows(index):
        return pl.ds(pl.multiple_of(index * block_len, block_len), block_len)

    def remote(src, dst, sems, index, ctx, ch):
        return pltpu.make_async_remote_copy(
            src_ref=src,
            dst_ref=dst,
            send_sem=sems.at[0, index],
            recv_sem=sems.at[1, index],
            device_id={"ctx": ctx, "ch": ch},
            device_id_type=MESH,
        )

    weight_steps = []
    for k in hops:
        target = lax.rem(z + k, lines) * 2
        weight_steps += [target + 1 - core, target + core]

    def weight_copy(step):
        slot = step % W_SLOTS
        start = pl.multiple_of(weight_steps[step] * chans, chans)
        return pltpu.make_async_copy(
            out_weight.at[pl.ds(start, chans), :], w_buf.at[slot], w_sem.at[slot]
        )

    for step in range(W_SLOTS):
        weight_copy(step).start()

    barrier = pltpu.get_barrier_semaphore()
    greeted = [(lax.rem(me_ctx + d, n_ctx), me_ch) for d in range(1, n_ctx)]
    greeted += [(me_ctx, lax.rem(z + d, lines) * 2 + core) for d in range(1, lines)]
    greeted.append((me_ctx, z * 2 + 1 - core))
    for ctx, ch in greeted:
        pl.semaphore_signal(
            barrier, inc=1, device_id={"ctx": ctx, "ch": ch}, device_id_type=MESH
        )

    def stage_filter(tile, carry):
        per_part = part // TILE
        filter_out[tile // per_part, :, column(lax.rem(tile, per_part))] = long_filter[
            :, column(tile)
        ]
        return carry

    lax.fori_loop(0, chans // TILE, stage_filter, 0)
    filter_wide[token_rows(me_ctx), :] = filter_out[me_ctx]
    pl.semaphore_wait(barrier, len(greeted))

    def exchange(number, src_at, dst):
        copies = []
        for distance in range(1, n_ctx):
            peer = lax.rem(me_ctx + distance, n_ctx)
            copies.append(
                remote(
                    src_at(peer),
                    dst,
                    exchange_sems.at[number],
                    distance - 1,
                    peer,
                    me_ch,
                )
            )
        for copy in copies:
            copy.start()
        return copies

    def arrived(copies):
        for copy in copies:
            copy.wait_recv()

    edge_copy = remote(
        features.at[:, pl.ds(block_len - EDGE, EDGE), :],
        edge_in,
        edge_sems,
        0,
        lax.rem(me_ctx + 1, n_ctx),
        me_ch,
    )
    edge_copy.start()
    filter_copies = exchange(0, lambda peer: filter_out.at[peer], filter_wide.at[token_rows(me_ctx)])

    pair_copies, line_copies = [], []

    def finish_hop(index):
        pair_copies[index].wait_recv()
        if hops[index] == 0:
            partials[index] = partials[index] + pair_in[index].astype(F32)
            return
        line_out[index] = (partials[index] + pair_in[index].astype(F32)).astype(BF16)
        copy = remote(
            line_out.at[index],
            line_in.at[index],
            line_sems,
            index,
            me_ctx,
            lax.rem(z + hops[index], lines) * 2 + core,
        )
        copy.start()
        line_copies.append(copy)

    for step in range(2 * lines):
        index = step // 2
        slot = step % W_SLOTS
        weight_copy(step).wait()

        def project(tile, carry, step=step, index=index, slot=slot):
            rows = pl.ds(pl.multiple_of(tile * ROWS, ROWS), ROWS)
            value = lax.dot_general(
                grad_out[...],
                w_buf[slot, rows, :],
                (((1,), (1,)), ((), ())),
                preferred_element_type=F32,
            )
            if step % 2 == 0:
                pair_out[index, :, rows] = value.astype(BF16)
            else:
                partials[index, :, rows] = value
            return carry

        lax.fori_loop(0, chans // ROWS, project, 0)
        if step + W_SLOTS < 2 * lines:
            weight_copy(step + W_SLOTS).start()
        if step % 2 == 0:
            copy = remote(
                pair_out.at[index], pair_in.at[index], pair_sems, index, me_ctx, z * 2 + 1 - core
            )
            copy.start()
            pair_copies.append(copy)
            if index >= 1:
                finish_hop(index - 1)

    edge_copy.wait_recv()

    def convolve(tile, carry):
        cols = column(tile)
        totals = []
        for branch in range(3):
            edge = edge_in[branch, :, cols].astype(F32)
            extended[branch, 0:EDGE, cols] = jnp.where(me_ctx > 0, edge, 0.0)
            extended[branch, EDGE : EDGE + block_len, cols] = features[branch, :, cols].astype(F32)
            total = None
            for tap in range(taps):
                term = (
                    short_kernel[branch, tap : tap + 1, cols]
                    * extended[branch, EDGE - tap : EDGE - tap + block_len, cols]
                )
                total = term if total is None else total + term
            conv[branch, :, cols] = total
            totals.append(total)
        per_part = part // TILE
        gated_out[tile // per_part, :, column(lax.rem(tile, per_part))] = (
            totals[1] * totals[2]
        ).astype(BF16)
        return carry

    lax.fori_loop(0, chans // TILE, convolve, 0)
    gated_copies = exchange(1, lambda peer: gated_out.at[peer], gated_wide.at[token_rows(me_ctx)])
    gated_wide[token_rows(me_ctx), :] = gated_out[me_ctx]
    finish_hop(lines - 1)
    own_grad_out = pltpu.make_async_copy(grad_out, all_grad_out.at[me_ctx], local_sem.at[0])
    own_grad_out.start()

    def transform(source, target):
        def body(tile, carry):
            rows = pl.ds(pl.multiple_of(tile * ROWS, ROWS), ROWS)
            target[rows, :] = to_spectrum(ahead_high[rows, :], ahead_low[rows, :], source[...])
            return carry

        lax.fori_loop(0, 2 * length // ROWS, body, 0)

    def multiply(first, second, conjugate):
        step_rows = 32

        def body(tile, carry):
            upper = pl.ds(pl.multiple_of(tile * step_rows, step_rows), step_rows)
            lower = pl.ds(pl.multiple_of(length + tile * step_rows, step_rows), step_rows)
            first_real, first_imag = first[upper, :], first[lower, :]
            second_real, second_imag = second[upper, :], second[lower, :]
            row = lax.broadcasted_iota(jnp.int32, first_real.shape, 0) + tile * step_rows
            edge = row == 0
            real_real = first_real * second_real
            imag_imag = first_imag * second_imag
            if conjugate:
                real_part = real_real + imag_imag
                imag_part = first_real * second_imag - first_imag * second_real
            else:
                real_part = real_real - imag_imag
                imag_part = first_real * second_imag + first_imag * second_real
            for rows, value in (
                (upper, jnp.where(edge, real_real, real_part)),
                (lower, jnp.where(edge, imag_imag, imag_part)),
            ):
                high = value.astype(BF16)
                prod_high[rows, :] = high
                prod_low[rows, :] = (value - high.astype(F32)).astype(BF16)
            return carry

        lax.fori_loop(0, length // step_rows, body, 0)

    def invert(target):
        def body(tile, carry):
            rows = token_rows(tile)
            high, low = back_high[rows, :], back_low[rows, :]
            target[tile] = (
                jnp.dot(high, prod_high[...], preferred_element_type=F32)
                + jnp.dot(low, prod_high[...], preferred_element_type=F32)
                + jnp.dot(high, prod_low[...], preferred_element_type=F32)
            ).astype(BF16)
            return carry

        lax.fori_loop(0, n_ctx, body, 0)

    arrived(filter_copies)
    transform(filter_wide, filter_spec)
    arrived(gated_copies)
    transform(gated_wide, gated_spec)
    multiply(filter_spec, gated_spec, False)
    invert(long_send)
    long_copies = exchange(2, lambda peer: long_send.at[peer], long_recv.at[me_ctx])
    long_recv[me_ctx] = long_send[me_ctx]
    grad_out_copies = exchange(3, lambda peer: grad_out, all_grad_out.at[me_ctx])

    arrived(long_copies)

    def per_part_view(ref, tile):
        per_part = part // TILE
        return ref[tile // per_part, :, column(lax.rem(tile, per_part))].astype(F32)

    def mix(tile, carry):
        cols = column(tile)
        line_mixed[z, :, cols] = (conv[0, :, cols] * per_part_view(long_recv, tile)).astype(BF16)
        return carry

    lax.fori_loop(0, chans // TILE, mix, 0)

    def chain_copy(sign, distance):
        block = line_mixed.at[z - sign * (distance - 1)]
        way = 0 if sign > 0 else 1
        return remote(
            block, block, chain_sems.at[way], distance - 1, me_ctx, (z + sign) * 2 + core
        )

    def chain_sends(sign, distance):
        first, after = z - sign * (distance - 1), z + sign
        inside = jnp.logical_and(first >= 0, first < lines)
        return jnp.logical_and(inside, jnp.logical_and(after >= 0, after < lines))

    def chain_receives(sign, distance):
        first = z - sign * distance
        return jnp.logical_and(first >= 0, first < lines)

    own_relay = pltpu.make_async_copy(
        line_mixed.at[me_ctx], all_mixed.at[core, me_ctx], local_sem.at[1]
    )

    def relay_copy(block):
        return pltpu.make_async_remote_copy(
            src_ref=line_mixed.at[block],
            dst_ref=all_mixed.at[core, me_ctx],
            send_sem=relay_sems.at[0, block],
            recv_sem=relay_sems.at[1, me_ctx],
            device_id={"ctx": block, "ch": me_ch},
            device_id_type=MESH,
        )

    def relay(block):
        @pl.when(block == me_ctx)
        def _():
            own_relay.start()

        @pl.when(block != me_ctx)
        def _():
            relay_copy(block).start()

    def chain_start(distance):
        for sign in (1, -1):

            @pl.when(chain_sends(sign, distance))
            def _(sign=sign):
                chain_copy(sign, distance).start()

    def chain_take(distance):
        for sign in (1, -1):

            @pl.when(chain_receives(sign, distance))
            def _(sign=sign):
                chain_copy(sign, distance).wait_recv()

        if distance + 1 < lines:
            chain_start(distance + 1)
        for sign in (1, -1):

            @pl.when(chain_receives(sign, distance))
            def _(sign=sign):
                relay(z - sign * distance)

    chain_start(1)
    relay(z)
    for copy in line_copies:
        copy.wait_recv()

    def take_grad(tile, carry):
        cols = column(tile)
        total = partials[lines - 1, :, cols]
        for index in range(lines - 1):
            total = total + line_in[index, :, cols].astype(F32)
        grad_conv[0, 0:block_len, cols] = total * per_part_view(long_recv, tile)
        per_part = part // TILE
        grad_long_out[tile // per_part, :, column(lax.rem(tile, per_part))] = (
            total * conv[0, :, cols]
        ).astype(BF16)
        return carry

    lax.fori_loop(0, chans // TILE, take_grad, 0)
    grad_copies = exchange(
        4, lambda peer: grad_long_out.at[peer], grad_wide.at[token_rows(me_ctx)]
    )
    grad_wide[token_rows(me_ctx), :] = grad_long_out[me_ctx]

    def tap_gradient(branches):
        def body(tile, carry):
            cols = column(tile)
            for branch in branches:
                values = grad_conv[branch, 0:block_len, cols]
                for tap in range(taps):
                    term = values * extended[branch, EDGE - tap : EDGE - tap + block_len, cols]
                    kernel_parts[me_ctx, branch, tap : tap + 1, cols] = jnp.sum(
                        term, axis=0, keepdims=True
                    )
                kernel_parts[me_ctx, branch, taps : taps + 1, cols] = jnp.zeros((1, TILE), F32)
            return carry

        return body

    lax.fori_loop(0, chans // TILE, tap_gradient((0,)), 0)
    chain_take(1)
    arrived(grad_copies)
    transform(grad_wide, grad_spec)
    multiply(filter_spec, grad_spec, True)
    invert(back_send)
    back_copies = exchange(5, lambda peer: back_send.at[peer], back_recv.at[me_ctx])
    back_recv[me_ctx] = back_send[me_ctx]
    multiply(gated_spec, grad_spec, True)
    invert(lag_send)
    lag_copies = exchange(6, lambda peer: lag_send.at[peer], lag_recv.at[me_ctx])
    lag_recv[me_ctx] = lag_send[me_ctx]
    for distance in range(2, lines - 1):
        chain_take(distance)
    arrived(back_copies)

    def conv_gradient(tile, carry):
        cols = column(tile)
        back = per_part_view(back_recv, tile)
        grad_conv[1, 0:block_len, cols] = back * conv[2, :, cols]
        grad_conv[2, 0:block_len, cols] = back * conv[1, :, cols]
        return carry

    lax.fori_loop(0, chans // TILE, conv_gradient, 0)
    next_copy = remote(
        grad_conv.at[:, pl.ds(0, NEXT_EDGE), :],
        next_edge_in,
        next_sems,
        0,
        lax.rem(me_ctx + n_ctx - 1, n_ctx),
        me_ch,
    )
    next_copy.start()

    chain_take(lines - 1)
    lax.fori_loop(0, chans // TILE, tap_gradient((1, 2)), 0)
    kernel_copies = exchange(7, lambda peer: kernel_parts.at[me_ctx], kernel_parts.at[me_ctx])
    next_copy.wait()

    forward_copies = []
    for source in range(n_ctx):
        @pl.when(me_ctx == source)
        def _():
            own_relay.wait()

        @pl.when(me_ctx != source)
        def _(source=source):
            slot = all_mixed.at[core, source]
            remote(line_mixed.at[0], slot, relay_sems, source, me_ctx, me_ch).wait_recv()

        copy = remote(
            all_mixed.at[core, source],
            all_mixed.at[core, source],
            forward_sems,
            source,
            me_ctx,
            z * 2 + 1 - core,
        )
        copy.start()
        forward_copies.append(copy)

    def feature_gradient(tile, carry):
        cols = column(tile)
        for branch in range(3):
            grad_conv[branch, block_len : block_len + NEXT_EDGE, cols] = jnp.where(
                me_ctx < n_ctx - 1, next_edge_in[branch, :, cols], 0.0
            )
            total = None
            for tap in range(taps):
                term = (
                    short_kernel[branch, tap : tap + 1, cols]
                    * grad_conv[branch, tap : tap + block_len, cols]
                )
                total = term if total is None else total + term
            grad_features[branch, :, cols] = total.astype(BF16)
        return carry

    lax.fori_loop(0, chans // TILE, feature_gradient, 0)

    arrived(lag_copies)

    def filter_gradient(tile, carry):
        grad_filter[:, column(tile)] = per_part_view(lag_recv, tile)
        return carry

    lax.fori_loop(0, chans // TILE, filter_gradient, 0)
    arrived(kernel_copies)
    total = kernel_parts[0]
    for index in range(1, n_ctx):
        total = total + kernel_parts[index]
    grad_kernel[...] = total[:, :taps, :]
    arrived(grad_out_copies)
    own_grad_out.wait()
    for copy in forward_copies:
        copy.wait()
    edge_copy.wait_send()
    for copies in (
        filter_copies,
        gated_copies,
        long_copies,
        grad_out_copies,
        grad_copies,
        back_copies,
        lag_copies,
        kernel_copies,
        pair_copies,
        line_copies,
    ):
        for copy in copies:
            copy.wait_send()
    for distance in range(1, lines):
        for sign in (1, -1):

            @pl.when(chain_sends(sign, distance))
            def _(sign=sign, distance=distance):
                chain_copy(sign, distance).wait_send()

    for block in range(lines):

        @pl.when(me_ctx != block)
        def _(block=block):
            relay_copy(block).wait_send()


def product_kernel(
    mixed_tile,
    all_grad_out,
    features_from,
    kernel_from,
    filter_from,
    grad_weight,
    features_to,
    kernel_to,
    filter_to,
    features_held,
    kernel_held,
    filter_held,
    sems,
):
    step, steps = pl.program_id(0), pl.num_programs(0)
    ways = [
        (features_from, features_held, features_to),
        (kernel_from, kernel_held, kernel_to),
        (filter_from, filter_held, filter_to),
    ]
    takes = [
        pltpu.make_async_copy(source, held, sems.at[0, index])
        for index, (source, held, _) in enumerate(ways)
    ]
    gives = [
        pltpu.make_async_copy(held, target, sems.at[1, index])
        for index, (_, held, target) in enumerate(ways)
    ]

    @pl.when(step == 0)
    def _():
        for copy in takes:
            copy.start()

    @pl.when(step == steps // 2)
    def _():
        for take, give in zip(takes, gives):
            take.wait()
            give.start()

    grad_weight[...] = lax.dot_general(
        mixed_tile[0],
        all_grad_out[...],
        (((0,), (0,)), ((), ())),
        preferred_element_type=F32,
    )

    @pl.when(step == steps - 1)
    def _():
        for copy in gives:
            copy.wait()


def fused(features, short_kernel, long_filter, out_weight, grad_out):
    block_len, chans = grad_out.shape
    taps = short_kernel.shape[1]
    n_ctx, lines = lax.axis_size("ctx"), lax.axis_size("ch") // 2
    part, length = chans // n_ctx, n_ctx * block_len
    tables = [jnp.asarray(table) for table in fourier_tables(length)]
    in_vmem = pl.BlockSpec(memory_space=pltpu.VMEM)
    in_place = pl.BlockSpec(memory_space=pl.ANY)
    staged = pltpu.VMEM((n_ctx, block_len, part), BF16)
    wide = pltpu.VMEM((length, part), BF16)
    spectra = pltpu.VMEM((2 * length, part), F32)
    blocks = pltpu.VMEM((lines, block_len, chans), BF16)
    scratch = [
        pltpu.VMEM((W_SLOTS, chans, chans), BF16),
        blocks,
        blocks,
        pltpu.VMEM((lines, block_len, chans), F32),
        blocks,
        blocks,
        pltpu.VMEM((3, EDGE, chans), BF16),
        pltpu.VMEM((3, EDGE + block_len, chans), F32),
        pltpu.VMEM((3, block_len, chans), F32),
        staged,
        staged,
        staged,
        wide,
        wide,
        wide,
        spectra,
        spectra,
        spectra,
        pltpu.VMEM((2 * length, part), BF16),
        pltpu.VMEM((2 * length, part), BF16),
        staged,
        staged,
        staged,
        staged,
        staged,
        staged,
        blocks,
        pltpu.VMEM((3, block_len + NEXT_EDGE, chans), F32),
        pltpu.VMEM((3, NEXT_EDGE, chans), F32),
        pltpu.VMEM((n_ctx, 3, taps + 1, chans), F32),
        pltpu.SemaphoreType.DMA((W_SLOTS,)),
        pltpu.SemaphoreType.DMA((2,)),
        pltpu.SemaphoreType.DMA((2, lines)),
        pltpu.SemaphoreType.DMA((2, lines)),
        pltpu.SemaphoreType.DMA((2, 1)),
        pltpu.SemaphoreType.DMA((2, 1)),
        pltpu.SemaphoreType.DMA((8, 2, n_ctx - 1)),
        pltpu.SemaphoreType.DMA((2, 2, lines - 1)),
        pltpu.SemaphoreType.DMA((2, lines)),
        pltpu.SemaphoreType.DMA((2, n_ctx)),
    ]
    grad_features, grad_kernel, grad_filter, all_grad_out, all_mixed = pl.pallas_call(
        fused_kernel,
        out_shape=[
            jax.ShapeDtypeStruct(features.shape, BF16),
            jax.ShapeDtypeStruct(short_kernel.shape, F32),
            jax.ShapeDtypeStruct(long_filter.shape, F32),
            jax.ShapeDtypeStruct((n_ctx, block_len, chans), BF16),
            jax.ShapeDtypeStruct((2, n_ctx, block_len, chans), BF16),
        ],
        in_specs=[in_vmem, in_vmem, in_vmem, in_place] + [in_vmem] * 5,
        out_specs=[in_vmem] * 5,
        scratch_shapes=scratch,
        compiler_params=pltpu.CompilerParams(
            collective_id=0, has_side_effects=True, vmem_limit_bytes=56 * 1024 * 1024
        ),
        cost_estimate=pl.CostEstimate(
            flops=8 * 10**9, bytes_accessed=28 * 2**20, transcendentals=0
        ),
    )(features, short_kernel, long_filter, out_weight, grad_out, *tables)
    per_half = chans // ROWS
    grad_weight, grad_features, grad_kernel, grad_filter = pl.pallas_call(
        product_kernel,
        grid=(2 * per_half,),
        out_shape=[
            jax.ShapeDtypeStruct((2 * chans, chans), F32),
            jax.ShapeDtypeStruct(grad_features.shape, BF16),
            jax.ShapeDtypeStruct(grad_kernel.shape, F32),
            jax.ShapeDtypeStruct(grad_filter.shape, F32),
        ],
        in_specs=[
            pl.BlockSpec((1, length, ROWS), lambda i: (i // per_half, 0, lax.rem(i, per_half))),
            pl.BlockSpec((length, chans), lambda i: (0, 0)),
            in_place,
            in_place,
            in_place,
        ],
        out_specs=[
            pl.BlockSpec((ROWS, chans), lambda i: (i, 0)),
            in_place,
            in_place,
            in_place,
        ],
        scratch_shapes=[
            pltpu.VMEM(grad_features.shape, BF16),
            pltpu.VMEM(grad_kernel.shape, F32),
            pltpu.VMEM(grad_filter.shape, F32),
            pltpu.SemaphoreType.DMA((2, 3)),
        ],
        compiler_params=pltpu.CompilerParams(vmem_limit_bytes=60 * 1024 * 1024),
        cost_estimate=pl.CostEstimate(
            flops=4 * 10**9, bytes_accessed=12 * 2**20, transcendentals=0
        ),
    )(
        all_mixed.reshape(2, length, chans),
        all_grad_out.reshape(length, chans),
        grad_features,
        grad_kernel,
        grad_filter,
    )
    return (grad_features, grad_kernel, grad_filter, grad_weight)


def solution(mesh):
    n_ctx, n_ch = mesh.shape["ctx"], mesh.shape["ch"]

    def local(features, short_kernel, long_filter, out_weight, grad_out):
        aligned = grad_out.shape[1] % (TILE * n_ctx) == 0 and grad_out.shape[1] % ROWS == 0
        body = fused if n_ch == 2 * n_ctx and aligned else plain
        return body(features, short_kernel, long_filter, out_weight, grad_out)

    return jax.shard_map(
        local,
        mesh=mesh,
        in_specs=(
            P(None, "ctx", "ch"),
            P(None, None, "ch"),
            P("ctx", "ch"),
            P(None, "ch"),
            P("ctx", "ch"),
        ),
        out_specs=(P(None, "ctx", "ch"), P(None, None, "ch"), P("ctx", "ch"), P("ctx", "ch")),
        check_vma=False,
    )
```
